512 devices in a mesh: row: 32 (over x, z_hi, core), col: 16 (over y, z_lo).
Axes of the slice: x: 4, y: 8, z: 8 (z_hi: 4, z_lo: 2; z = z_hi * 2 + z_lo), core: 2. Of those that a mesh axis runs over, the one named last changes fastest.
Arguments:
- electric_x: float32 [192, 512, 128], P('col', 'row'), may hold values from -6 to 6
- electric_y: float32 [192, 512, 128], P('col', 'row'), may hold values from -6 to 6
- electric_z: float32 [192, 512, 128], P('col', 'row'), may hold values from -6 to 6
- magnetic_x: float32 [192, 512, 128], P('col', 'row'), may hold values from -6 to 6
- magnetic_y: float32 [192, 512, 128], P('col', 'row'), may hold values from -6 to 6
- magnetic_z: float32 [192, 512, 128], P('col', 'row'), may hold values from -6 to 6
- tissue: int32 [192, 512, 128], P('col', 'row'), may hold values from 0 to 63
- permittivity: float32 [64], replicated, may hold values from 1 to 60
- conductivity: float32 [64], replicated, may hold values from 0 to 1.5
Outputs:
- next_ex: float32 [192, 512, 128], P('col', 'row')
- next_ey: float32 [192, 512, 128], P('col', 'row')
- next_ez: float32 [192, 512, 128], P('col', 'row')
- next_hx: float32 [192, 512, 128], P('col', 'row')
- next_hy: float32 [192, 512, 128], P('col', 'row')
- next_hz: float32 [192, 512, 128], P('col', 'row')
The draws below stay inside these ranges and needn't reach their ends.
All inputs are finite; a program needn't handle non-finite values.
Results may differ from the reference program's by a relative error of at most 0.0003.
Values sent between devices are 32-bit elements; how exact they have to be, the bound alone decides.
A program may use at most 64 MiB of HBM per device.

```python
import math
import jax
import jax.numpy as jnp
from jax import lax

NX = 128
NT = 64
NY = 512
NZ = 192


def touch_ends(values, key, smallest, high):
    shape = values.shape
    place = [jax.random.randint(jax.random.fold_in(key, axis), (), 0, shape[axis]) for axis in range(len(shape))]
    values = values.at[tuple(place)].set(smallest)
    longest = shape.index(max(shape))
    place[longest] = (place[longest] + 1) % shape[longest]
    return values.at[tuple(place)].set(high)


def block_levels(stream_key, extent, cuts, smallest, largest):
    gain = 1.0
    for axis_at, shards_of in cuts:
        steps = jax.random.uniform(jax.random.fold_in(jax.random.fold_in(stream_key, 6), axis_at), (shards_of,), jnp.float32, smallest / len(cuts), largest / len(cuts))
        gain = gain * jnp.repeat(jnp.exp(steps), extent[axis_at] // shards_of).reshape((-1,) + (1,) * (len(extent) - 1 - axis_at))
    return gain


def centred(stream_key, shape, spread, most, split=(), held_as=jnp.bfloat16):
    gain = block_levels(stream_key, shape, split, -0.22, 0.18) if split else 1.0
    values = jax.random.normal(stream_key, shape, jnp.float32) * spread * gain
    return jnp.minimum(jnp.maximum(values, -most), most).astype(held_as)


def setup_inputs(seed: int = 0) -> dict:
    splits = jax.random.split(jax.random.key(seed), 10)
    return {
        "electric_x": centred(splits[0], (NZ, NY, NX), 1.0, 6.0, ((0, 16), (1, 32)), jnp.float32),
        "electric_y": centred(splits[1], (NZ, NY, NX), 1.0, 6.0, ((0, 16), (1, 32)), jnp.float32),
        "electric_z": centred(splits[2], (NZ, NY, NX), 1.0, 6.0, ((0, 16), (1, 32)), jnp.float32),
        "magnetic_x": centred(splits[3], (NZ, NY, NX), 1.0, 6.0, ((0, 16), (1, 32)), jnp.float32),
        "magnetic_y": centred(splits[4], (NZ, NY, NX), 1.0, 6.0, ((0, 16), (1, 32)), jnp.float32),
        "magnetic_z": centred(splits[5], (NZ, NY, NX), 1.0, 6.0, ((0, 16), (1, 32)), jnp.float32),
        "tissue": touch_ends(jax.random.randint(splits[6], (NZ, NY, NX), 0, NT), jax.random.fold_in(splits[6], 1), 0, NT - 1).astype(jnp.int32),
        "permittivity": jnp.clip(jnp.exp(jax.random.uniform(splits[7], (NT,), jnp.float32, math.log(1.0), math.log(60.0))), 1.0, 60.0),
        "conductivity": jnp.clip(jax.random.uniform(splits[8], (NT,), jnp.float32, 0.0, 1.5), 0.0, 1.5),
    }


half_step = 32.0


def ahead_diff(grid_field, dim_index):
    widths = [(0, 1) if which_dim == dim_index else (0, 0) for which_dim in range(3)]
    padded = jnp.pad(grid_field, widths)
    return lax.slice_in_dim(padded, 1, None, axis=dim_index) - grid_field


def behind_diff(grid_field, dim_index):
    widths = [(1, 0) if which_dim == dim_index else (0, 0) for which_dim in range(3)]
    padded = jnp.pad(grid_field, widths)
    return grid_field - lax.slice_in_dim(padded, 0, grid_field.shape[dim_index], axis=dim_index)


def material(eps_cell, sig_cell):
    denom_cell = eps_cell + sig_cell * (0.5 * half_step)
    keep_factor = (eps_cell - sig_cell * (0.5 * half_step)) / denom_cell
    curl_factor = half_step / denom_cell
    coupling = curl_factor * half_step
    return keep_factor, curl_factor, coupling


def thomas_lines(coupling, source):
    full_shape = source.shape
    line_count = full_shape[0]
    coupling = coupling.reshape(line_count, -1)
    source = source.reshape(line_count, -1)
    position = lax.broadcasted_iota(jnp.int32, source.shape, 0)
    lower = jnp.where(position == 0, 0.0, -coupling)
    upper = jnp.where(position == line_count - 1, 0.0, -coupling)
    middle = jnp.where(position == 0, 1.0 + coupling, 1.0 + 2.0 * coupling)

    def sweep_down(carried, entries):
        prev_up, prev_val = carried
        low_e, mid_e, up_e, src_e = entries
        denom_v = mid_e - low_e * prev_up
        new_up = up_e / denom_v
        new_val = (src_e - low_e * prev_val) / denom_v
        return (new_up, new_val), (new_up, new_val)

    zeros_b = jnp.zeros(source.shape[1:], source.dtype)
    ignored, (ups_all, vals_all) = lax.scan(sweep_down, (zeros_b, zeros_b), (lower, middle, upper, source))

    def sweep_up(after_v, entries):
        up_e, val_e = entries
        result = val_e - up_e * after_v
        return result, result

    ignored, solved = lax.scan(sweep_up, zeros_b, (ups_all, vals_all), reverse=True)
    return solved.reshape(full_shape)


def solve_along(coupling, source, dim_index):
    moved = thomas_lines(jnp.moveaxis(coupling, dim_index, 0), jnp.moveaxis(source, dim_index, 0))
    return jnp.moveaxis(moved, 0, dim_index)


def reference(electric_x, electric_y, electric_z, magnetic_x, magnetic_y, magnetic_z, tissue, permittivity, conductivity):
    keep_factor, curl_factor, coupling = material(permittivity[tissue], conductivity[tissue])
    source_x = keep_factor * electric_x + curl_factor * (behind_diff(magnetic_z, 1) - behind_diff(magnetic_y, 0)) - coupling * behind_diff(ahead_diff(electric_y, 2), 1)
    source_y = keep_factor * electric_y + curl_factor * (behind_diff(magnetic_x, 0) - behind_diff(magnetic_z, 2)) - coupling * behind_diff(ahead_diff(electric_z, 1), 0)
    source_z = keep_factor * electric_z + curl_factor * (behind_diff(magnetic_y, 2) - behind_diff(magnetic_x, 1)) - coupling * behind_diff(ahead_diff(electric_x, 0), 2)
    half_ex = solve_along(coupling, source_x, 1)
    half_ey = solve_along(coupling, source_y, 0)
    half_ez = solve_along(coupling, source_z, 2)
    half_hx = magnetic_x + half_step * (ahead_diff(half_ey, 0) - ahead_diff(electric_z, 1))
    half_hy = magnetic_y + half_step * (ahead_diff(half_ez, 2) - ahead_diff(electric_x, 0))
    half_hz = magnetic_z + half_step * (ahead_diff(half_ex, 1) - ahead_diff(electric_y, 2))
    second_x = keep_factor * half_ex + curl_factor * (behind_diff(half_hz, 1) - behind_diff(half_hy, 0)) - coupling * behind_diff(ahead_diff(half_ez, 2), 0)
    second_y = keep_factor * half_ey + curl_factor * (behind_diff(half_hx, 0) - behind_diff(half_hz, 2)) - coupling * behind_diff(ahead_diff(half_ex, 1), 2)
    second_z = keep_factor * half_ez + curl_factor * (behind_diff(half_hy, 2) - behind_diff(half_hx, 1)) - coupling * behind_diff(ahead_diff(half_ey, 0), 1)
    next_ex = solve_along(coupling, second_x, 0)
    next_ey = solve_along(coupling, second_y, 2)
    next_ez = solve_along(coupling, second_z, 1)
    next_hx = half_hx + half_step * (ahead_diff(half_ey, 0) - ahead_diff(next_ez, 1))
    next_hy = half_hy + half_step * (ahead_diff(half_ez, 2) - ahead_diff(next_ex, 0))
    next_hz = half_hz + half_step * (ahead_diff(half_ex, 1) - ahead_diff(next_ey, 2))
    return (next_ex, next_ey, next_ez, next_hx, next_hy, next_hz)
```

```python
import functools

import jax
import jax.numpy as jnp
from jax import lax
from jax.experimental import pallas as pl
from jax.experimental.pallas import tpu as pltpu
from jax.sharding import PartitionSpec as P

MESH = pl.DeviceIdType.MESH
half_step = 32.0
inv_half = 1.0 / half_step
TILE = 8


def roll(values, shift, axis):
    return pltpu.roll(values, shift, axis)


def cyclic_setup(low, up, diag, axis, keep):
    n = diag.shape[axis]
    stride = 1
    level = 0
    while stride < n:
        inv = 1.0 / diag
        from_low = low * roll(inv, stride, axis)
        from_up = up * roll(inv, n - stride, axis)
        diag = diag - from_low * low - from_up * up
        if 2 * stride < n:
            low = from_low * roll(low, stride, axis)
            up = from_up * roll(up, n - stride, axis)
        keep(2 * level, from_low)
        keep(2 * level + 1, from_up)
        stride, level = 2 * stride, level + 1
    keep(2 * level, 1.0 / diag)


def cyclic_solve(rhs, axis, kept):
    n = rhs.shape[axis]
    stride = 1
    level = 0
    while stride < n:
        rhs = (
            rhs
            + kept(2 * level) * roll(rhs, stride, axis)
            + kept(2 * level + 1) * roll(rhs, n - stride, axis)
        )
        stride, level = 2 * stride, level + 1
    return rhs * kept(2 * level)


def levels_of(n):
    return (n - 1).bit_length()


def kernel(sizes, *refs):
    lz, ly, nx, nrow, ncol, nt = sizes
    cells = lz * ly
    (ex_h, ey_h, ez_h, mx_h, my_h, mz_h, tis_h, eps_s, sig_s) = refs[:9]
    (nex, ney, nez, nhx, nhy, nhz) = refs[9:15]
    (
        ex, ey, ez, mx, my, mz, tis,
        recip, keepf, ax, ay, az,
        fx, fy, fz, ex1, ey1, ez1, dex, dey, dez, cx, cy, cz,
        sh0, sh1, sh2, sh3,
        xfac,
        uy, ry, vy, uz, rz, vz,
        send_y, send_z, gat_y, gat_z, ret_y, ret_z, res_y, res_z,
        fac_y, fac_z, mid_y, mid_z,
        halo_mx_s, halo_ez_s, halo_mx, halo_ez, halo_my, halo_ex,
        load_sem, halo_send, halo_recv, sems,
    ) = refs[15:]

    me_r, me_c = lax.axis_index("row"), lax.axis_index("col")
    gate_r = jnp.where(me_r > 0, 1.0, 0.0)
    gate_c = jnp.where(me_c > 0, 1.0, 0.0)
    gate_r_end = jnp.where(me_r < nrow - 1, 1.0, 0.0)
    gate_c_end = jnp.where(me_c < ncol - 1, 1.0, 0.0)

    def at_row(p):
        return (p, me_c)

    def at_col(p):
        return (me_r, p)

    loads = [
        pltpu.make_async_copy(src, dst, load_sem.at[i])
        for i, (src, dst) in enumerate(
            ((tis_h, tis), (mx_h, mx), (ez_h, ez), (my_h, my), (ex_h, ex), (ey_h, ey), (mz_h, mz))
        )
    ]
    for load in loads:
        load.start()

    barrier = pltpu.get_barrier_semaphore()

    def greet_row(i, _):
        pl.semaphore_signal(
            barrier, inc=1, device_id=at_row(lax.rem(me_r + 1 + i, nrow)), device_id_type=MESH
        )
        return 0

    def greet_col(i, _):
        pl.semaphore_signal(
            barrier, inc=1, device_id=at_col(lax.rem(me_c + 1 + i, ncol)), device_id_type=MESH
        )
        return 0

    lax.fori_loop(0, nrow - 1, greet_row, 0)
    lax.fori_loop(0, ncol - 1, greet_col, 0)

    loads[0].wait()
    part = cells // 2
    group = 4

    def look_up(c, _):
        at = pl.ds(pl.multiple_of(c * part, 8), part)
        label = tis[at, :]

        def tissues(g, carry):
            eps, sig = carry
            for j in range(group):
                t = g * group + j
                same = label == t
                eps = jnp.where(same, eps_s[t], eps)
                sig = jnp.where(same, sig_s[t], sig)
            return eps, sig

        zero = jnp.zeros(label.shape, jnp.float32)
        eps, sig = lax.fori_loop(0, nt // group, tissues, (zero, zero))
        loss = sig * (0.5 * half_step)
        scale = inv_half * inv_half
        recip[at, :] = (eps + loss) * scale
        keepf[at, :] = (eps - loss) * scale
        return 0

    lax.fori_loop(0, 2, look_up, 0)

    for load in loads[1:]:
        load.wait()

    def row_y(ref, i):
        return ref[pl.ds(i, lz, stride=ly), :]

    def put_y(ref, i, values):
        ref[pl.ds(i, lz, stride=ly), :] = values

    def row_z(ref, i):
        return ref[pl.ds(i * ly, ly), :]

    def put_z(ref, i, values):
        ref[pl.ds(i * ly, ly), :] = values

    halo_mx_s[pl.ds(0, lz), :] = row_y(mx, ly - 1)
    halo_ez_s[pl.ds(0, lz), :] = row_y(ez, 0)
    pl.semaphore_wait(barrier, nrow + ncol - 2)

    up_r, down_r = lax.rem(me_r + 1, nrow), lax.rem(me_r + nrow - 1, nrow)
    up_c, down_c = lax.rem(me_c + 1, ncol), lax.rem(me_c + ncol - 1, ncol)

    def remote(src, dst, send_sem, recv_sem, device):
        return pltpu.make_async_remote_copy(
            src_ref=src,
            dst_ref=dst,
            send_sem=send_sem,
            recv_sem=recv_sem,
            device_id=device,
            device_id_type=MESH,
        )

    halos = [
        remote(halo_mx_s, halo_mx, halo_send.at[0], halo_recv.at[0], at_row(up_r)),
        remote(halo_ez_s, halo_ez, halo_send.at[1], halo_recv.at[1], at_row(down_r)),
        remote(my.at[pl.ds(cells - ly, ly), :], halo_my, halo_send.at[2], halo_recv.at[2], at_col(up_c)),
        remote(ex.at[pl.ds(0, ly), :], halo_ex, halo_send.at[3], halo_recv.at[3], at_col(down_c)),
    ]
    for halo in halos:
        halo.start()

    def matrix_forward(n, row, first_gate, u_ref, r_ref, send, count):
        diag = row(recip, 0) + (2.0 - first_gate)
        inv = 1.0 / diag
        reach = inv
        beta = reach
        u_ref[0], r_ref[0] = reach, inv
        for i in range(1, n - 1):
            diag = row(recip, i) + 2.0 - inv
            inv = 1.0 / diag
            further = reach * inv
            beta = beta + reach * further
            reach = further
            u_ref[i], r_ref[i] = reach, inv
        send[pl.ds(0, count, stride=TILE), :] = row(recip, n - 1) + 2.0 - inv
        send[pl.ds(1, count, stride=TILE), :] = beta
        send[pl.ds(2, count, stride=TILE), :] = reach

    def rhs_forward(n, row, f_ref, u_ref, r_ref, v_ref, send, count, passed_on):
        value = row(f_ref, 0) * r_ref[0]
        psi = value
        v_ref[0] = value
        for i in range(1, n - 1):
            value = (row(f_ref, i) + value) * r_ref[i]
            psi = psi + u_ref[i - 1] * value
            v_ref[i] = value
        send[pl.ds(3, count, stride=TILE), :] = row(f_ref, n - 1) + value
        send[pl.ds(4, count, stride=TILE), :] = psi
        send[pl.ds(5, count, stride=TILE), :] = passed_on

    def back(n, row_put, u_ref, r_ref, v_ref, got, count, out, diff):
        before = got[pl.ds(0, count, stride=TILE), :] + got[pl.ds(3, count, stride=TILE), :]
        value = got[pl.ds(1, count, stride=TILE), :]
        row_put(out, n - 1, value)
        row_put(diff, n - 1, got[pl.ds(2, count, stride=TILE), :] - value)
        for i in range(n - 2, -1, -1):
            lower = (v_ref[i] + u_ref[i] * before) + r_ref[i] * value
            row_put(out, i, lower)
            row_put(diff, i, value - lower)
            value = lower

    first_r, first_c = 1.0 - gate_r, 1.0 - gate_c
    matrix_forward(ly, row_y, first_r, uy, ry, send_y, lz)
    matrix_forward(lz, row_z, first_c, uz, rz, send_z, ly)

    chunk = 32 if cells % 32 == 0 else 8

    def x_setup(c, _):
        at = pl.multiple_of(c * chunk, 8)
        diag = recip[pl.ds(at, chunk), :]
        lane = lax.broadcasted_iota(jnp.int32, diag.shape, 1)
        low = jnp.where(lane == 0, 0.0, 1.0)
        up = jnp.where(lane == nx - 1, 0.0, 1.0)

        def keep(slot, values):
            xfac[slot, pl.ds(at, chunk), :] = values

        cyclic_setup(low, up, diag + 1.0 + low, 1, keep)
        return 0

    lax.fori_loop(0, cells // chunk, x_setup, 0)

    lane = lax.broadcasted_iota(jnp.int32, (cells, nx), 1)

    def before_x(values):
        return jnp.where(lane == 0, 0.0, roll(values, 1, 1))

    def after_x(values):
        return jnp.where(lane == nx - 1, 0.0, roll(values, nx - 1, 1))

    def before_y(values, first, shifted):
        shifted[...] = roll(values, 1, 0)
        put_y(shifted, 0, first)
        return shifted[...]

    def after_y(values, last, shifted):
        shifted[...] = roll(values, cells - 1, 0)
        put_y(shifted, ly - 1, last)
        return shifted[...]

    def before_z(values, first):
        return jnp.concatenate([first, values[: cells - ly]], axis=0)

    def after_z(values, last):
        return jnp.concatenate([values[ly:], last], axis=0)

    def x_solve(f_ref, write):
        def lines(c, _):
            at = pl.multiple_of(c * chunk, 8)
            solved = cyclic_solve(
                f_ref[pl.ds(at, chunk), :], 1, lambda slot: xfac[slot, pl.ds(at, chunk), :]
            )
            column = lax.broadcasted_iota(jnp.int32, solved.shape, 1)
            ahead = jnp.where(column == nx - 1, 0.0, roll(solved, nx - 1, 1)) - solved
            write(pl.ds(at, chunk), solved, ahead)
            return 0

        lax.fori_loop(0, cells // chunk, lines, 0)

    zero_y = jnp.zeros((lz, nx), jnp.float32)
    zero_z = jnp.zeros((ly, nx), jnp.float32)

    mz_v = mz[...]
    ey_v = ey[...]
    ay_v = mz_v * inv_half - (after_x(ey_v) - ey_v)
    ay[...] = ay_v
    for halo in halos:
        halo.wait_recv()
    my_v = my[...]
    my_before = before_z(my_v, halo_my[...] * gate_c)
    fx[...] = (
        keepf[...] * ex[...] - (my_v - my_before) * inv_half + (ay_v - before_y(ay_v, zero_y, sh0))
    )
    ez_v = ez[...]
    mx_v = mx[...]
    ez_after = after_y(ez_v, halo_ez[pl.ds(0, lz), :] * gate_r_end, sh1)
    az_v = mx_v * inv_half - (ez_after - ez_v)
    az[...] = az_v
    fy[...] = (
        keepf[...] * ey_v - (mz_v - before_x(mz_v)) * inv_half + (az_v - before_z(az_v, zero_z))
    )

    me_owner_j = lax.div(lz * me_r + nrow - 1, nrow)

    def owner_of(j):
        return lax.div(j * nrow, lz)

    owns = jnp.logical_and(me_owner_j < lz, owner_of(me_owner_j) == me_r)
    others = jnp.logical_not(owns)

    def tile(ref, i):
        return ref.at[pl.ds(pl.multiple_of(i * TILE, TILE), TILE), :]

    def wait_send(ref, count, sem):
        part_of = ref.at[pl.ds(0, count * TILE), :]
        remote(part_of, part_of, sem, sem, at_row(up_r)).wait_send()

    def wait_recv(ref, count, sem):
        part_of = ref.at[pl.ds(0, count * TILE), :]
        remote(part_of, part_of, sem, sem, at_row(up_r)).wait_recv()

    def scatter_y(step):
        def to_owner(i, _):
            j = lax.rem(me_r + i, lz)
            owner = owner_of(j)

            @pl.when(owner != me_r)
            def _():
                remote(
                    tile(send_y, j), tile(gat_y.at[step], me_r), sems.at[0, step], sems.at[1, step], at_row(owner)
                ).start()

            return 0

        lax.fori_loop(0, lz, to_owner, 0)

        @pl.when(owns)
        def _():
            gat_y[step, pl.ds(pl.multiple_of(me_r * TILE, TILE), TILE), :] = send_y[
                pl.ds(pl.multiple_of(me_owner_j * TILE, TILE), TILE), :
            ]

    def scatter_z(step):
        def to_owner(i, _):
            q = lax.rem(me_c + 1 + i, ncol)
            remote(
                tile(send_z, q), tile(gat_z.at[step], me_c), sems.at[2, step], sems.at[3, step], at_col(q)
            ).start()
            return 0

        lax.fori_loop(0, ncol - 1, to_owner, 0)
        own = pl.ds(pl.multiple_of(me_c * TILE, TILE), TILE)
        gat_z[step, own, :] = send_z[own, :]

    def solve_owned(step, n, got, fac, mid, ret):
        def read(r):
            return got[step, pl.ds(r, n, stride=TILE), :]

        place = lax.broadcasted_iota(jnp.int32, (n, nx), 0)
        starts, ends = place == 0, place == n - 1
        if step == 0:
            beta = read(1)
            link = jnp.where(starts, 0.0, read(2))
            beta_up = jnp.where(ends, 0.0, roll(beta, n - 1, 0))
            link_up = jnp.where(ends, 0.0, roll(link, n - 1, 0))
            mid[0], mid[1], mid[2], mid[3] = beta, link, beta_up, link_up

            def keep(slot, values):
                fac[slot] = values

            cyclic_setup(link, link_up, read(0) - beta_up, 0, keep)
        else:
            beta, link, beta_up, link_up = mid[0], mid[1], mid[2], mid[3]
        added = jnp.where(starts, 0.0, roll(read(5), 1, 0))
        phi = read(3) + link * added
        psi = read(4) + beta * added
        psi_up = jnp.where(ends, 0.0, roll(psi, n - 1, 0))
        last = cyclic_solve(phi + psi_up, 0, lambda slot: fac[slot])
        before = jnp.where(starts, 0.0, roll(last, 1, 0))
        after = psi_up + beta_up * last + link_up * roll(last, n - 1, 0)
        ret[step, pl.ds(0, n, stride=TILE), :] = before
        ret[step, pl.ds(1, n, stride=TILE), :] = last
        ret[step, pl.ds(2, n, stride=TILE), :] = after
        ret[step, pl.ds(3, n, stride=TILE), :] = added

    def own_y(step):
        @pl.when(owns)
        def _():
            wait_recv(gat_y.at[step], nrow - 1, sems.at[1, step])
            solve_owned(step, nrow, gat_y, fac_y, mid_y, ret_y)

            def give(i, _):
                q = lax.rem(me_r + 1 + i, nrow)
                remote(
                    tile(ret_y.at[step], q), tile(res_y.at[step], me_owner_j), sems.at[4, step], sems.at[5, step], at_row(q)
                ).start()
                return 0

            lax.fori_loop(0, nrow - 1, give, 0)
            res_y[step, pl.ds(pl.multiple_of(me_owner_j * TILE, TILE), TILE), :] = ret_y[
                step, pl.ds(pl.multiple_of(me_r * TILE, TILE), TILE), :
            ]

    def own_z(step):
        wait_recv(gat_z.at[step], ncol - 1, sems.at[3, step])
        solve_owned(step, ncol, gat_z, fac_z, mid_z, ret_z)

        def give(i, _):
            q = lax.rem(me_c + 1 + i, ncol)
            remote(
                tile(ret_z.at[step], q), tile(res_z.at[step], me_c), sems.at[6, step], sems.at[7, step], at_col(q)
            ).start()
            return 0

        lax.fori_loop(0, ncol - 1, give, 0)
        own = pl.ds(pl.multiple_of(me_c * TILE, TILE), TILE)
        res_z[step, own, :] = ret_z[step, own, :]

    def wait_sent(step):
        @pl.when(owns)
        def _():
            wait_send(send_y, lz - 1, sems.at[0, step])
            wait_send(ret_y.at[step], nrow - 1, sems.at[4, step])

        @pl.when(others)
        def _():
            wait_send(send_y, lz, sems.at[0, step])

        wait_send(send_z, ncol - 1, sems.at[2, step])
        wait_send(ret_z.at[step], ncol - 1, sems.at[6, step])

    def wait_y(step):
        @pl.when(owns)
        def _():
            wait_recv(res_y.at[step], lz - 1, sems.at[5, step])

        @pl.when(others)
        def _():
            wait_recv(res_y.at[step], lz, sems.at[5, step])

    def wait_z(step):
        wait_recv(res_z.at[step], ncol - 1, sems.at[7, step])

    rhs_forward(ly, row_y, fx, uy, ry, vy, send_y, lz, -row_y(ay, ly - 1))
    scatter_y(0)
    rhs_forward(lz, row_z, fy, uz, rz, vz, send_z, ly, -row_z(az, lz - 1))
    scatter_z(0)

    ex_v = ex[...]
    ax_v = my[...] * inv_half - (after_z(ex_v, halo_ex[...] * gate_c_end) - ex_v)
    ax[...] = ax_v
    mx_v = mx[...]
    mx_before = before_y(mx_v, halo_mx[pl.ds(0, lz), :] * gate_r, sh2)
    fz[...] = (
        keepf[...] * ez[...] - (mx_v - mx_before) * inv_half + (ax_v - before_x(ax_v))
    )

    def keep_half(at, solved, ahead):
        ez1[at, :] = solved
        dez[at, :] = ahead

    x_solve(fz, keep_half)
    cz_v = ax[...] + 2.0 * dez[...]
    cz[...] = cz_v
    hy_v = ax[...] + dez[...]
    fz[...] = keepf[...] * ez1[...] + (hy_v - before_x(hy_v))
    fx[...] = before_z(cz_v, zero_z) - cz_v

    own_z(0)
    own_y(0)
    wait_sent(0)

    wait_z(0)
    back(lz, put_z, uz, rz, vz, res_z.at[0], ly, ey1, dey)
    wait_y(0)
    back(ly, put_y, uy, ry, vy, res_y.at[0], lz, ex1, dex)

    dex_v, dey_v = dex[...], dey[...]
    ay_v, az_v = ay[...], az[...]
    cx_v, cy_v = ay_v + 2.0 * dex_v, az_v + 2.0 * dey_v
    cx[...], cy[...] = cx_v, cy_v
    hz_v = ay_v + dex_v
    hz_first = (
        row_y(ex1, 0) - res_y[0, pl.ds(0, lz, stride=TILE), :] - res_y[0, pl.ds(3, lz, stride=TILE), :]
    ) * gate_r
    fx[...] = fx[...] + keepf[...] * ex1[...] + (hz_v - before_y(hz_v, hz_first, sh0))
    fz[...] = fz[...] - (cy_v - before_y(cy_v, zero_y, sh1))

    rhs_forward(ly, row_y, fz, uy, ry, vy, send_y, lz, row_y(cy, ly - 1))
    scatter_y(1)
    rhs_forward(lz, row_z, fx, uz, rz, vz, send_z, ly, row_z(cz, lz - 1))
    scatter_z(1)

    hx_v = az[...] + dey[...]
    hx_first = (
        row_z(ey1, 0) - res_z[0, pl.ds(0, ly, stride=TILE), :] - res_z[0, pl.ds(3, ly, stride=TILE), :]
    ) * gate_c
    cx_v = cx[...]
    fy[...] = keepf[...] * ey1[...] + (hx_v - before_z(hx_v, hx_first)) - (cx_v - before_x(cx_v))

    def write_y(at, solved, ahead):
        ney[at, :] = solved
        nhz[at, :] = (cx[at, :] - ahead) * half_step

    x_solve(fy, write_y)

    own_z(1)
    own_y(1)
    wait_z(1)
    back(lz, put_z, uz, rz, vz, res_z.at[1], ly, nex, dez)
    nhy[...] = (cz[...] - dez[...]) * half_step
    wait_y(1)
    back(ly, put_y, uy, ry, vy, res_y.at[1], lz, nez, dex)
    nhx[...] = (cy[...] - dex[...]) * half_step
    wait_sent(1)
    for halo in halos:
        halo.wait_send()


def solution(mesh):
    nrow, ncol = mesh.shape["row"], mesh.shape["col"]

    def per_device(ex, ey, ez, mx, my, mz, tissue, permittivity, conductivity):
        lz, ly, nx = ex.shape
        cells, nt = lz * ly, permittivity.shape[0]
        f32 = jnp.float32
        flat = [a.reshape(cells, nx) for a in (ex, ey, ez, mx, my, mz, tissue)]
        whole = pltpu.VMEM((cells, nx), f32)
        pad_z = -(-lz // 8) * 8
        slots = lambda n: 2 * levels_of(n) + 1
        scratch = (
            [whole] * 6
            + [pltpu.VMEM((cells, nx), jnp.int32)]
            + [whole] * 21
            + [pltpu.VMEM((slots(nx), cells, nx), f32)]
            + [pltpu.VMEM((ly - 1, lz, nx), f32)] * 3
            + [pltpu.VMEM((lz - 1, ly, nx), f32)] * 3
            + [pltpu.VMEM((lz * TILE, nx), f32), pltpu.VMEM((ly * TILE, nx), f32)]
            + [pltpu.VMEM((2, nrow * TILE, nx), f32), pltpu.VMEM((2, ncol * TILE, nx), f32)] * 2
            + [pltpu.VMEM((2, lz * TILE, nx), f32), pltpu.VMEM((2, ly * TILE, nx), f32)]
            + [pltpu.VMEM((slots(nrow), nrow, nx), f32), pltpu.VMEM((slots(ncol), ncol, nx), f32)]
            + [pltpu.VMEM((4, nrow, nx), f32), pltpu.VMEM((4, ncol, nx), f32)]
            + [pltpu.VMEM((pad_z, nx), f32)] * 4
            + [pltpu.VMEM((ly, nx), f32)] * 2
            + [
                pltpu.SemaphoreType.DMA((7,)),
                pltpu.SemaphoreType.DMA((4,)),
                pltpu.SemaphoreType.DMA((4,)),
                pltpu.SemaphoreType.DMA((8, 2)),
            ]
        )
        outs = pl.pallas_call(
            functools.partial(kernel, (lz, ly, nx, nrow, ncol, nt)),
            out_shape=[jax.ShapeDtypeStruct((cells, nx), f32)] * 6,
            in_specs=[pl.BlockSpec(memory_space=pl.ANY)] * 7 + [pl.BlockSpec(memory_space=pltpu.SMEM)] * 2,
            out_specs=[pl.BlockSpec(memory_space=pltpu.VMEM)] * 6,
            scratch_shapes=scratch,
            compiler_params=pltpu.CompilerParams(
                collective_id=0, has_side_effects=True, vmem_limit_bytes=32 * 1024 * 1024
            ),
        )(*flat, permittivity, conductivity)
        return tuple(o.reshape(lz, ly, nx) for o in outs)

    cut = P("col", "row", None)
    return jax.shard_map(
        per_device,
        mesh=mesh,
        in_specs=(cut,) * 7 + (P(), P()),
        out_specs=(cut,) * 6,
        check_vma=False,
    )
```

```python
import functools

import jax
import jax.numpy as jnp
from jax import lax
from jax.experimental import pallas as pl
from jax.experimental.pallas import tpu as pltpu
from jax.sharding import PartitionSpec as P

MESH = pl.DeviceIdType.MESH
half_step = 32.0
inv_half = 1.0 / half_step
TILE = 8
VMEM_BYTES = 56 * 1024 * 1024


def roll(values, shift, axis):
    return pltpu.roll(values, shift, axis)


def cyclic_setup(low, up, excess, axis, keep):
    n = excess.shape[axis]
    stride = 1
    level = 0
    while stride < n:
        inv = 1.0 / (low + up + excess)
        from_low = low * roll(inv, stride, axis)
        from_up = up * roll(inv, n - stride, axis)
        excess = (
            excess
            + from_low * roll(excess, stride, axis)
            + from_up * roll(excess, n - stride, axis)
        )
        if 2 * stride < n:
            low = from_low * roll(low, stride, axis)
            up = from_up * roll(up, n - stride, axis)
        keep(2 * level, from_low)
        keep(2 * level + 1, from_up)
        stride, level = 2 * stride, level + 1
    keep(2 * level, 1.0 / excess)


def cyclic_solve(rhs, axis, kept):
    n = rhs.shape[axis]
    stride = 1
    level = 0
    while stride < n:
        rhs = (
            rhs
            + kept(2 * level) * roll(rhs, stride, axis)
            + kept(2 * level + 1) * roll(rhs, n - stride, axis)
        )
        stride, level = 2 * stride, level + 1
    return rhs * kept(2 * level)


def levels_of(n):
    return (n - 1).bit_length()


def kernel(sizes, *refs):
    lz, ly, nx, nrow, ncol, nt = sizes
    cells = lz * ly
    (ex_h, ey_h, ez_h, mx_h, my_h, mz_h, tis_h, eps_h, sig_h) = refs[:9]
    outs_h = refs[9:15]
    (
        eps_s, sig_s,
        ex, ey, ez, mx, my, mz, tis,
        nex, ney, nez, nhx, nhy, nhz,
        recip, keepf, twice, gx, gy, gz, ax, ay, az,
        fx, fy, fz, ex1, ey1, ez1, dex, dey, dez, cx, cy, cz,
        sh0, sh1, sh2, sh3,
        xfac,
        uy, ry, vy, uz, rz, vz,
        send_y0, send_y1, send_z0, send_z1, gat_y, gat_z, ret_y, ret_z, res_y, res_z,
        fac_y, fac_z, mid_y, mid_z,
        halo_mx_s, halo_ez_s, halo_mx, halo_ez, halo_my, halo_ex,
        load_sem, store_sem, halo_send, halo_recv, sems,
    ) = refs[15:]

    me_r, me_c = lax.axis_index("row"), lax.axis_index("col")
    gate_r = jnp.where(me_r > 0, 1.0, 0.0)
    gate_c = jnp.where(me_c > 0, 1.0, 0.0)
    gate_r_end = jnp.where(me_r < nrow - 1, 1.0, 0.0)
    gate_c_end = jnp.where(me_c < ncol - 1, 1.0, 0.0)

    def at_row(p):
        return (p, me_c)

    def at_col(p):
        return (me_r, p)

    loads = [
        pltpu.make_async_copy(src, dst, load_sem.at[i])
        for i, (src, dst) in enumerate(
            (
                (eps_h, eps_s),
                (sig_h, sig_s),
                (tis_h, tis),
                (mx_h, mx),
                (ez_h, ez),
                (my_h, my),
                (ex_h, ex),
                (ey_h, ey),
                (mz_h, mz),
            )
        )
    ]
    for load in loads:
        load.start()

    stores = [
        pltpu.make_async_copy(src, dst, store_sem.at[i])
        for i, (src, dst) in enumerate(zip((nex, ney, nez, nhx, nhy, nhz), outs_h))
    ]

    def store(*which):
        for i in which:
            stores[i].start()

    barrier = pltpu.get_barrier_semaphore()

    def greet_row(i, _):
        pl.semaphore_signal(
            barrier, inc=1, device_id=at_row(lax.rem(me_r + 1 + i, nrow)), device_id_type=MESH
        )
        return 0

    def greet_col(i, _):
        pl.semaphore_signal(
            barrier, inc=1, device_id=at_col(lax.rem(me_c + 1 + i, ncol)), device_id_type=MESH
        )
        return 0

    lax.fori_loop(0, nrow - 1, greet_row, 0)
    lax.fori_loop(0, ncol - 1, greet_col, 0)

    for load in loads[:3]:
        load.wait()
    part = cells // 2
    group = 4

    def look_up(c, _):
        at = pl.ds(pl.multiple_of(c * part, 8), part)
        label = tis[at, :]

        def tissues(g, carry):
            eps, sig = carry
            for j in range(group):
                t = g * group + j
                same = label == t
                eps = jnp.where(same, eps_s[t], eps)
                sig = jnp.where(same, sig_s[t], sig)
            return eps, sig

        zero = jnp.zeros(label.shape, jnp.float32)
        eps, sig = lax.fori_loop(0, nt // group, tissues, (zero, zero))
        loss = sig * (0.5 * half_step)
        scale = inv_half * inv_half
        recip[at, :] = (eps + loss) * scale
        keepf[at, :] = (eps - loss) * scale
        twice[at, :] = eps * (2.0 * scale)
        return 0

    lax.fori_loop(0, 2, look_up, 0)

    for load in loads[3:]:
        load.wait()

    def row_y(ref, i):
        return ref[pl.ds(i, lz, stride=ly), :]

    def put_y(ref, i, values):
        ref[pl.ds(i, lz, stride=ly), :] = values

    def row_z(ref, i):
        return ref[pl.ds(i * ly, ly), :]

    def put_z(ref, i, values):
        ref[pl.ds(i * ly, ly), :] = values

    halo_mx_s[pl.ds(0, lz), :] = row_y(mx, ly - 1)
    halo_ez_s[pl.ds(0, lz), :] = row_y(ez, 0)
    pl.semaphore_wait(barrier, nrow + ncol - 2)

    up_r, down_r = lax.rem(me_r + 1, nrow), lax.rem(me_r + nrow - 1, nrow)
    up_c, down_c = lax.rem(me_c + 1, ncol), lax.rem(me_c + ncol - 1, ncol)

    def remote(src, dst, send_sem, recv_sem, device):
        return pltpu.make_async_remote_copy(
            src_ref=src,
            dst_ref=dst,
            send_sem=send_sem,
            recv_sem=recv_sem,
            device_id=device,
            device_id_type=MESH,
        )

    halos = [
        remote(my.at[pl.ds(cells - ly, ly), :], halo_my, halo_send.at[0], halo_recv.at[0], at_col(up_c)),
        remote(halo_ez_s, halo_ez, halo_send.at[1], halo_recv.at[1], at_row(down_r)),
        remote(halo_mx_s, halo_mx, halo_send.at[2], halo_recv.at[2], at_row(up_r)),
        remote(ex.at[pl.ds(0, ly), :], halo_ex, halo_send.at[3], halo_recv.at[3], at_col(down_c)),
    ]
    for halo in halos:
        halo.start()

    def matrix_forward(n, row, gate, u_ref, r_ref, send, count):
        share = row(recip, 0)
        rest = share + gate
        inv = 1.0 / (1.0 + rest)
        reach = inv
        gain = share * inv
        beta, gains = reach, gain
        u_ref[0], r_ref[0] = reach, inv
        for i in range(1, n - 1):
            share = row(recip, i)
            rest = share + rest * inv
            inv = 1.0 / (1.0 + rest)
            gain = (share + gain) * inv
            gains = gains + reach * gain
            further = reach * inv
            beta = beta + reach * further
            reach = further
            u_ref[i], r_ref[i] = reach, inv
        send[pl.ds(0, count, stride=TILE), :] = row(recip, n - 1) + gain
        send[pl.ds(1, count, stride=TILE), :] = gains
        send[pl.ds(2, count, stride=TILE), :] = reach
        send[pl.ds(6, count, stride=TILE), :] = beta

    def rhs_forward(n, row, f_ref, u_ref, r_ref, v_ref, send, count, passed_on):
        value = row(f_ref, 0) * r_ref[0]
        psi = value
        v_ref[0] = value
        for i in range(1, n - 1):
            value = (row(f_ref, i) + value) * r_ref[i]
            psi = psi + u_ref[i - 1] * value
            v_ref[i] = value
        send[pl.ds(3, count, stride=TILE), :] = row(f_ref, n - 1) + value
        send[pl.ds(4, count, stride=TILE), :] = psi
        send[pl.ds(5, count, stride=TILE), :] = passed_on

    def back(n, row_put, u_ref, r_ref, v_ref, got, count, out, diff):
        before = got[pl.ds(0, count, stride=TILE), :]
        value = got[pl.ds(1, count, stride=TILE), :]
        row_put(out, n - 1, value)
        row_put(diff, n - 1, got[pl.ds(2, count, stride=TILE), :] - value)
        for i in range(n - 2, -1, -1):
            lower = (v_ref[i] + u_ref[i] * before) + r_ref[i] * value
            row_put(out, i, lower)
            row_put(diff, i, value - lower)
            value = lower

    matrix_forward(ly, row_y, gate_r, uy, ry, send_y0, lz)
    matrix_forward(lz, row_z, gate_c, uz, rz, send_z0, ly)

    chunk = 32 if cells % 32 == 0 else 8

    def x_setup(c, _):
        at = pl.multiple_of(c * chunk, 8)
        excess = recip[pl.ds(at, chunk), :]
        lane = lax.broadcasted_iota(jnp.int32, excess.shape, 1)
        low = jnp.where(lane == 0, 0.0, 1.0)
        up = jnp.where(lane == nx - 1, 0.0, 1.0)

        def keep(slot, values):
            xfac[slot, pl.ds(at, chunk), :] = values

        cyclic_setup(low, up, excess + (1.0 - up), 1, keep)
        return 0

    lax.fori_loop(0, cells // chunk, x_setup, 0)

    lane = lax.broadcasted_iota(jnp.int32, (cells, nx), 1)

    def before_x(values):
        return jnp.where(lane == 0, 0.0, roll(values, 1, 1))

    def after_x(values):
        return jnp.where(lane == nx - 1, 0.0, roll(values, nx - 1, 1))

    def before_y(values, first, shifted):
        shifted[...] = roll(values, 1, 0)
        put_y(shifted, 0, first)
        return shifted[...]

    def after_y(values, last, shifted):
        shifted[...] = roll(values, cells - 1, 0)
        put_y(shifted, ly - 1, last)
        return shifted[...]

    def before_z(values, first):
        return jnp.concatenate([first, values[: cells - ly]], axis=0)

    def after_z(values, last):
        return jnp.concatenate([values[ly:], last], axis=0)

    def x_solve(f_ref, write):
        def lines(c, _):
            at = pl.multiple_of(c * chunk, 8)
            solved = cyclic_solve(
                f_ref[pl.ds(at, chunk), :], 1, lambda slot: xfac[slot, pl.ds(at, chunk), :]
            )
            column = lax.broadcasted_iota(jnp.int32, solved.shape, 1)
            ahead = jnp.where(column == nx - 1, 0.0, roll(solved, nx - 1, 1)) - solved
            write(pl.ds(at, chunk), solved, ahead)
            return 0

        lax.fori_loop(0, cells // chunk, lines, 0)

    zero_y = jnp.zeros((lz, nx), jnp.float32)
    zero_z = jnp.zeros((ly, nx), jnp.float32)

    mz_v = mz[...]
    ey_v = ey[...]
    ay_v = mz_v * inv_half - (after_x(ey_v) - ey_v)
    ay[...] = ay_v
    halos[0].wait_recv()
    my_v = my[...]
    my_before = before_z(my_v, halo_my[...] * gate_c)
    gx_v = keepf[...] * ex[...] - (my_v - my_before) * inv_half
    gx[...] = gx_v
    fx[...] = gx_v + (ay_v - before_y(ay_v, zero_y, sh0))
    me_owner_j = lax.div(lz * me_r + nrow - 1, nrow)

    def owner_of(j):
        return lax.div(j * nrow, lz)

    owns = jnp.logical_and(me_owner_j < lz, owner_of(me_owner_j) == me_r)
    others = jnp.logical_not(owns)

    def for_each(count, body):
        half = count // 2

        def pair(k, _):
            body(half + k, 0)
            body(half - 1 - k, 0)
            return 0

        lax.fori_loop(0, half, pair, 0)
        if count % 2:
            body(count - 1, 0)

    def tile(ref, i):
        return ref.at[pl.ds(pl.multiple_of(i * TILE, TILE), TILE), :]

    def wait_send(ref, count, sem):
        part_of = ref.at[pl.ds(0, count * TILE), :]
        remote(part_of, part_of, sem, sem, at_row(up_r)).wait_send()

    def wait_recv(ref, count, sem):
        part_of = ref.at[pl.ds(0, count * TILE), :]
        remote(part_of, part_of, sem, sem, at_row(up_r)).wait_recv()

    sends_y, sends_z = (send_y0, send_y1), (send_z0, send_z1)

    def scatter_y(step):
        send_y = sends_y[step]

        def to_owner(i, _):
            j = lax.rem(me_r + i, lz)
            owner = owner_of(j)

            @pl.when(owner != me_r)
            def _():
                remote(
                    tile(send_y, j), tile(gat_y.at[step], me_r), sems.at[0, step], sems.at[1, step], at_row(owner)
                ).start()

            return 0

        lax.fori_loop(0, lz, to_owner, 0)

        @pl.when(owns)
        def _():
            gat_y[step, pl.ds(pl.multiple_of(me_r * TILE, TILE), TILE), :] = send_y[
                pl.ds(pl.multiple_of(me_owner_j * TILE, TILE), TILE), :
            ]

    def scatter_z(step):
        send_z = sends_z[step]

        def to_owner(i, _):
            q = lax.rem(me_c + 1 + i, ncol)
            remote(
                tile(send_z, q), tile(gat_z.at[step], me_c), sems.at[2, step], sems.at[3, step], at_col(q)
            ).start()
            return 0

        for_each(ncol - 1, to_owner)
        own = pl.ds(pl.multiple_of(me_c * TILE, TILE), TILE)
        gat_z[step, own, :] = send_z[own, :]

    def solve_owned(step, n, got, fac, mid, ret):
        def read(r):
            return got[step, pl.ds(r, n, stride=TILE), :]

        place = lax.broadcasted_iota(jnp.int32, (n, nx), 0)
        starts, ends = place == 0, place == n - 1
        if step == 0:
            beta = read(6)
            link = jnp.where(starts, 0.0, read(2))
            beta_up = jnp.where(ends, 0.0, roll(beta, n - 1, 0))
            link_up = jnp.where(ends, 0.0, roll(link, n - 1, 0))
            mid[0], mid[1], mid[2], mid[3] = beta, link, beta_up, link_up

            def keep(slot, values):
                fac[slot] = values

            excess = read(0) + jnp.where(ends, 1.0, roll(read(1), n - 1, 0))
            cyclic_setup(link, link_up, excess, 0, keep)
        else:
            beta, link, beta_up, link_up = mid[0], mid[1], mid[2], mid[3]
        added = jnp.where(starts, 0.0, roll(read(5), 1, 0))
        phi = read(3) + link * added
        psi = read(4) + beta * added
        psi_up = jnp.where(ends, 0.0, roll(psi, n - 1, 0))
        last = cyclic_solve(phi + psi_up, 0, lambda slot: fac[slot])
        before = jnp.where(starts, 0.0, roll(last, 1, 0)) + added
        after = psi_up + beta_up * last + link_up * roll(last, n - 1, 0)
        ret[step, pl.ds(0, n, stride=TILE), :] = before
        ret[step, pl.ds(1, n, stride=TILE), :] = last
        ret[step, pl.ds(2, n, stride=TILE), :] = after

    def own_y(step):
        @pl.when(owns)
        def _():
            wait_recv(gat_y.at[step], nrow - 1, sems.at[1, step])
            solve_owned(step, nrow, gat_y, fac_y, mid_y, ret_y)

            def give(i, _):
                q = lax.rem(me_r + 1 + i, nrow)
                remote(
                    tile(ret_y.at[step], q), tile(res_y.at[step], me_owner_j), sems.at[4, step], sems.at[5, step], at_row(q)
                ).start()
                return 0

            for_each(nrow - 1, give)
            res_y[step, pl.ds(pl.multiple_of(me_owner_j * TILE, TILE), TILE), :] = ret_y[
                step, pl.ds(pl.multiple_of(me_r * TILE, TILE), TILE), :
            ]

    def own_z(step):
        wait_recv(gat_z.at[step], ncol - 1, sems.at[3, step])
        solve_owned(step, ncol, gat_z, fac_z, mid_z, ret_z)

        def give(i, _):
            q = lax.rem(me_c + 1 + i, ncol)
            remote(
                tile(ret_z.at[step], q), tile(res_z.at[step], me_c), sems.at[6, step], sems.at[7, step], at_col(q)
            ).start()
            return 0

        for_each(ncol - 1, give)
        own = pl.ds(pl.multiple_of(me_c * TILE, TILE), TILE)
        res_z[step, own, :] = ret_z[step, own, :]

    def wait_sent(step):
        send_y, send_z = sends_y[step], sends_z[step]

        @pl.when(owns)
        def _():
            wait_send(send_y, lz - 1, sems.at[0, step])
            wait_send(ret_y.at[step], nrow - 1, sems.at[4, step])

        @pl.when(others)
        def _():
            wait_send(send_y, lz, sems.at[0, step])

        wait_send(send_z, ncol - 1, sems.at[2, step])
        wait_send(ret_z.at[step], ncol - 1, sems.at[6, step])

    def wait_y(step):
        @pl.when(owns)
        def _():
            wait_recv(res_y.at[step], lz - 1, sems.at[5, step])

        @pl.when(others)
        def _():
            wait_recv(res_y.at[step], lz, sems.at[5, step])

    def wait_z(step):
        wait_recv(res_z.at[step], ncol - 1, sems.at[7, step])

    rhs_forward(ly, row_y, fx, uy, ry, vy, send_y0, lz, -row_y(ay, ly - 1))
    scatter_y(0)
    halos[1].wait_recv()
    ez_v = ez[...]
    mx_v = mx[...]
    ez_after = after_y(ez_v, halo_ez[pl.ds(0, lz), :] * gate_r_end, sh1)
    az_v = mx_v * inv_half - (ez_after - ez_v)
    az[...] = az_v
    gy_v = keepf[...] * ey_v - (mz_v - before_x(mz_v)) * inv_half
    gy[...] = gy_v
    fy[...] = gy_v + (az_v - before_z(az_v, zero_z))
    rhs_forward(lz, row_z, fy, uz, rz, vz, send_z0, ly, -row_z(az, lz - 1))
    scatter_z(0)

    halos[2].wait_recv()
    halos[3].wait_recv()
    ex_v = ex[...]
    ax_v = my[...] * inv_half - (after_z(ex_v, halo_ex[...] * gate_c_end) - ex_v)
    ax[...] = ax_v
    mx_v = mx[...]
    mx_before = before_y(mx_v, halo_mx[pl.ds(0, lz), :] * gate_r, sh2)
    gz_v = keepf[...] * ez[...] - (mx_v - mx_before) * inv_half
    gz[...] = gz_v
    fz[...] = gz_v + (ax_v - before_x(ax_v))

    def keep_half(at, solved, ahead):
        ez1[at, :] = solved
        dez[at, :] = ahead

    x_solve(fz, keep_half)
    cz_v = ax[...] + 2.0 * dez[...]
    cz[...] = cz_v
    fz[...] = twice[...] * ez1[...] - gz[...]
    fx[...] = (before_z(cz_v, zero_z) - cz_v) - gx[...]

    own_z(0)
    own_y(0)
    wait_z(0)
    back(lz, put_z, uz, rz, vz, res_z.at[0], ly, ey1, dey)
    wait_y(0)
    back(ly, put_y, uy, ry, vy, res_y.at[0], lz, ex1, dex)

    cx_v = ay[...] + 2.0 * dex[...]
    cy_v = az[...] + 2.0 * dey[...]
    cx[...], cy[...] = cx_v, cy_v
    fz[...] = fz[...] - (cy_v - before_y(cy_v, zero_y, sh1))
    fx[...] = fx[...] + twice[...] * ex1[...]

    rhs_forward(ly, row_y, fz, uy, ry, vy, send_y1, lz, row_y(cy, ly - 1))
    scatter_y(1)
    rhs_forward(lz, row_z, fx, uz, rz, vz, send_z1, ly, row_z(cz, lz - 1))
    scatter_z(1)

    cx_v = cx[...]
    fy[...] = (twice[...] * ey1[...] - gy[...]) - (cx_v - before_x(cx_v))

    def write_y(at, solved, ahead):
        ney[at, :] = solved
        nhz[at, :] = (cx[at, :] - ahead) * half_step

    x_solve(fy, write_y)
    store(1, 5)

    own_z(1)
    own_y(1)
    wait_z(1)
    back(lz, put_z, uz, rz, vz, res_z.at[1], ly, nex, dez)
    nhy[...] = (cz[...] - dez[...]) * half_step
    store(0, 4)
    wait_y(1)
    back(ly, put_y, uy, ry, vy, res_y.at[1], lz, nez, dex)
    nhx[...] = (cy[...] - dex[...]) * half_step
    store(2, 3)
    wait_sent(0)
    wait_sent(1)
    for halo in halos:
        halo.wait_send()
    for done in stores:
        done.wait()


def deliver(*refs):
    sem = refs[12]
    copies = [
        pltpu.make_async_copy(src, dst, sem.at[i])
        for i, (src, dst) in enumerate(zip(refs[:6], refs[6:12]))
    ]
    for copy in copies:
        copy.start()
    for copy in copies:
        copy.wait()


def solution(mesh):
    nrow, ncol = mesh.shape["row"], mesh.shape["col"]

    def per_device(ex, ey, ez, mx, my, mz, tissue, permittivity, conductivity):
        lz, ly, nx = ex.shape
        cells, nt = lz * ly, permittivity.shape[0]
        f32 = jnp.float32
        flat = [a.reshape(cells, nx) for a in (ex, ey, ez, mx, my, mz, tissue)]
        whole = pltpu.VMEM((cells, nx), f32)
        pad_z = -(-lz // 8) * 8
        slots = lambda n: 2 * levels_of(n) + 1
        scratch = (
            [pltpu.SMEM((nt,), f32)] * 2
            + [whole] * 6
            + [pltpu.VMEM((cells, nx), jnp.int32)]
            + [whole] * 31
            + [pltpu.VMEM((slots(nx), cells, nx), f32)]
            + [pltpu.VMEM((ly - 1, lz, nx), f32)] * 3
            + [pltpu.VMEM((lz - 1, ly, nx), f32)] * 3
            + [pltpu.VMEM((lz * TILE, nx), f32)] * 2 + [pltpu.VMEM((ly * TILE, nx), f32)] * 2
            + [pltpu.VMEM((2, nrow * TILE, nx), f32), pltpu.VMEM((2, ncol * TILE, nx), f32)] * 2
            + [pltpu.VMEM((2, lz * TILE, nx), f32), pltpu.VMEM((2, ly * TILE, nx), f32)]
            + [pltpu.VMEM((slots(nrow), nrow, nx), f32), pltpu.VMEM((slots(ncol), ncol, nx), f32)]
            + [pltpu.VMEM((4, nrow, nx), f32), pltpu.VMEM((4, ncol, nx), f32)]
            + [pltpu.VMEM((pad_z, nx), f32)] * 4
            + [pltpu.VMEM((ly, nx), f32)] * 2
            + [
                pltpu.SemaphoreType.DMA((9,)),
                pltpu.SemaphoreType.DMA((6,)),
                pltpu.SemaphoreType.DMA((4,)),
                pltpu.SemaphoreType.DMA((4,)),
                pltpu.SemaphoreType.DMA((8, 2)),
            ]
        )
        outs = pl.pallas_call(
            functools.partial(kernel, (lz, ly, nx, nrow, ncol, nt)),
            out_shape=[jax.ShapeDtypeStruct((cells, nx), f32)] * 6,
            in_specs=[pl.BlockSpec(memory_space=pltpu.HBM)] * 9,
            out_specs=[pl.BlockSpec(memory_space=pltpu.HBM)] * 6,
            scratch_shapes=scratch,
            compiler_params=pltpu.CompilerParams(
                collective_id=0, has_side_effects=True, vmem_limit_bytes=VMEM_BYTES
            ),
        )(*flat, permittivity, conductivity)
        outs = pl.pallas_call(
            deliver,
            out_shape=[jax.ShapeDtypeStruct((cells, nx), f32)] * 6,
            in_specs=[pl.BlockSpec(memory_space=pltpu.HBM)] * 6,
            out_specs=[pl.BlockSpec(memory_space=pltpu.HBM)] * 6,
            scratch_shapes=[pltpu.SemaphoreType.DMA((6,))],
            compiler_params=pltpu.CompilerParams(vmem_limit_bytes=VMEM_BYTES),
        )(*outs)
        return tuple(o.reshape(lz, ly, nx) for o in outs)

    cut = P("col", "row", None)
    return jax.shard_map(
        per_device,
        mesh=mesh,
        in_specs=(cut,) * 7 + (P(), P()),
        out_specs=(cut,) * 6,
        check_vma=False,
    )
```

```python
import functools

import jax
import jax.numpy as jnp
from jax import lax
from jax.experimental import pallas as pl
from jax.experimental.pallas import tpu as pltpu
from jax.sharding import PartitionSpec as P

MESH = pl.DeviceIdType.MESH
half_step = 32.0
inv_half = 1.0 / half_step
TILE = 4
VMEM_BYTES = 56 * 1024 * 1024


def roll(values, shift, axis):
    return pltpu.roll(values, shift, axis)


def cyclic_setup(low, up, excess, axis, keep):
    n = excess.shape[axis]
    stride = 1
    level = 0
    while stride < n:
        inv = 1.0 / (low + up + excess)
        from_low = low * roll(inv, stride, axis)
        from_up = up * roll(inv, n - stride, axis)
        excess = (
            excess
            + from_low * roll(excess, stride, axis)
            + from_up * roll(excess, n - stride, axis)
        )
        if 2 * stride < n:
            low = from_low * roll(low, stride, axis)
            up = from_up * roll(up, n - stride, axis)
        keep(2 * level, from_low)
        keep(2 * level + 1, from_up)
        stride, level = 2 * stride, level + 1
    keep(2 * level, 1.0 / excess)


def cyclic_solve(rhs, axis, kept):
    n = rhs.shape[axis]
    stride = 1
    level = 0
    while stride < n:
        rhs = (
            rhs
            + kept(2 * level) * roll(rhs, stride, axis)
            + kept(2 * level + 1) * roll(rhs, n - stride, axis)
        )
        stride, level = 2 * stride, level + 1
    return rhs * kept(2 * level)


def levels_of(n):
    return (n - 1).bit_length()


def kernel(sizes, *refs):
    lz, ly, nx, nrow, ncol, nt = sizes
    cells = lz * ly
    (ex_h, ey_h, ez_h, mx_h, my_h, mz_h, tis_h, eps_h, sig_h) = refs[:9]
    outs_h = refs[9:15]
    (
        eps_s, sig_s,
        ex, ey, ez, mx, my, mz, tis,
        nex, ney, nez, nhx, nhy, nhz,
        recip, keepf, twice, gx, gy, gz, ax, ay, az,
        fx, fy, fz, ex1, ey1, ez1, dex, dey, dez, cx, cy, cz,
        sh0, sh1, sh2, sh3,
        xfac,
        uy, ry, vy, uz, rz, vz,
        send_y0, send_y1, send_ym, send_z0, send_z1, send_zm, gat_y, gat_z, ret_y, ret_z, res_y, res_z,
        fac_y, fac_z, mid_y, mid_z,
        halo_mx_s, halo_ez_s, halo_mx, halo_ez, halo_my, halo_ex,
        load_sem, store_sem, halo_send, halo_recv, sems,
    ) = refs[15:]

    me_r, me_c = lax.axis_index("row"), lax.axis_index("col")
    gate_r = jnp.where(me_r > 0, 1.0, 0.0)
    gate_c = jnp.where(me_c > 0, 1.0, 0.0)
    gate_r_end = jnp.where(me_r < nrow - 1, 1.0, 0.0)
    gate_c_end = jnp.where(me_c < ncol - 1, 1.0, 0.0)

    def at_row(p):
        return (p, me_c)

    def at_col(p):
        return (me_r, p)

    loads = [
        pltpu.make_async_copy(src, dst, load_sem.at[i])
        for i, (src, dst) in enumerate(
            (
                (eps_h, eps_s),
                (sig_h, sig_s),
                (tis_h, tis),
                (mx_h, mx),
                (ez_h, ez),
                (my_h, my),
                (ex_h, ex),
                (ey_h, ey),
                (mz_h, mz),
            )
        )
    ]
    for load in loads:
        load.start()

    stores = [
        pltpu.make_async_copy(src, dst, store_sem.at[i])
        for i, (src, dst) in enumerate(zip((nex, ney, nez, nhx, nhy, nhz), outs_h))
    ]

    def store(*which):
        for i in which:
            stores[i].start()

    barrier = pltpu.get_barrier_semaphore()

    def greet_row(i, _):
        pl.semaphore_signal(
            barrier, inc=1, device_id=at_row(lax.rem(me_r + 1 + i, nrow)), device_id_type=MESH
        )
        return 0

    def greet_col(i, _):
        pl.semaphore_signal(
            barrier, inc=1, device_id=at_col(lax.rem(me_c + 1 + i, ncol)), device_id_type=MESH
        )
        return 0

    lax.fori_loop(0, nrow - 1, greet_row, 0)
    lax.fori_loop(0, ncol - 1, greet_col, 0)

    for load in loads[:3]:
        load.wait()
    part = cells // 2
    group = 4

    def look_up(c, _):
        at = pl.ds(pl.multiple_of(c * part, 8), part)
        label = tis[at, :]

        def tissues(g, carry):
            eps, sig = carry
            for j in range(group):
                t = g * group + j
                same = label == t
                eps = jnp.where(same, eps_s[t], eps)
                sig = jnp.where(same, sig_s[t], sig)
            return eps, sig

        zero = jnp.zeros(label.shape, jnp.float32)
        eps, sig = lax.fori_loop(0, nt // group, tissues, (zero, zero))
        loss = sig * (0.5 * half_step)
        scale = inv_half * inv_half
        recip[at, :] = (eps + loss) * scale
        keepf[at, :] = (eps - loss) * scale
        twice[at, :] = eps * (2.0 * scale)
        return 0

    lax.fori_loop(0, 2, look_up, 0)

    for load in loads[3:]:
        load.wait()

    def row_y(ref, i):
        return ref[pl.ds(i, lz, stride=ly), :]

    def put_y(ref, i, values):
        ref[pl.ds(i, lz, stride=ly), :] = values

    def row_z(ref, i):
        return ref[pl.ds(i * ly, ly), :]

    def put_z(ref, i, values):
        ref[pl.ds(i * ly, ly), :] = values

    def matrix_forward(n, row, gate, u_ref, r_ref, send):
        share = row(recip, 0)
        rest = share + gate
        inv = 1.0 / (1.0 + rest)
        reach = inv
        gain = share * inv
        beta, gains = reach, gain
        u_ref[0], r_ref[0] = reach, inv
        for i in range(1, n - 1):
            share = row(recip, i)
            rest = share + rest * inv
            inv = 1.0 / (1.0 + rest)
            gain = (share + gain) * inv
            gains = gains + reach * gain
            further = reach * inv
            beta = beta + reach * further
            reach = further
            u_ref[i], r_ref[i] = reach, inv
        send[:, 0, :] = row(recip, n - 1) + gain
        send[:, 1, :] = gains
        send[:, 2, :] = reach
        send[:, 3, :] = beta

    matrix_forward(ly, row_y, gate_r, uy, ry, send_ym)
    matrix_forward(lz, row_z, gate_c, uz, rz, send_zm)

    halo_mx_s[pl.ds(0, lz), :] = row_y(mx, ly - 1)
    halo_ez_s[pl.ds(0, lz), :] = row_y(ez, 0)
    pl.semaphore_wait(barrier, nrow + ncol - 2)

    up_r, down_r = lax.rem(me_r + 1, nrow), lax.rem(me_r + nrow - 1, nrow)
    up_c, down_c = lax.rem(me_c + 1, ncol), lax.rem(me_c + ncol - 1, ncol)

    def remote(src, dst, send_sem, recv_sem, device):
        return pltpu.make_async_remote_copy(
            src_ref=src,
            dst_ref=dst,
            send_sem=send_sem,
            recv_sem=recv_sem,
            device_id=device,
            device_id_type=MESH,
        )

    halos = [
        remote(my.at[pl.ds(cells - ly, ly), :], halo_my, halo_send.at[0], halo_recv.at[0], at_col(up_c)),
        remote(halo_ez_s, halo_ez, halo_send.at[1], halo_recv.at[1], at_row(down_r)),
        remote(halo_mx_s, halo_mx, halo_send.at[2], halo_recv.at[2], at_row(up_r)),
        remote(ex.at[pl.ds(0, ly), :], halo_ex, halo_send.at[3], halo_recv.at[3], at_col(down_c)),
    ]
    for halo in halos:
        halo.start()

    def rhs_forward(n, row, f_ref, u_ref, r_ref, v_ref, send, passed_on):
        value = row(f_ref, 0) * r_ref[0]
        psi = value
        v_ref[0] = value
        for i in range(1, n - 1):
            value = (row(f_ref, i) + value) * r_ref[i]
            psi = psi + u_ref[i - 1] * value
            v_ref[i] = value
        send[:, 0, :] = row(f_ref, n - 1) + value
        send[:, 1, :] = psi
        send[:, 2, :] = passed_on

    def back(n, row_put, u_ref, r_ref, v_ref, got, out, diff):
        before = got[:, 0, :]
        value = got[:, 1, :]
        row_put(out, n - 1, value)
        row_put(diff, n - 1, got[:, 2, :] - value)
        for i in range(n - 2, -1, -1):
            lower = (v_ref[i] + u_ref[i] * before) + r_ref[i] * value
            row_put(out, i, lower)
            row_put(diff, i, value - lower)
            value = lower


    me_owner_j = lax.div(lz * me_r + nrow - 1, nrow)

    def owner_of(j):
        return lax.div(j * nrow, lz)

    owns = jnp.logical_and(me_owner_j < lz, owner_of(me_owner_j) == me_r)
    others = jnp.logical_not(owns)

    def for_each(count, body):
        half = count // 2

        def pair(k, _):
            body(half + k, 0)
            body(half - 1 - k, 0)
            return 0

        lax.fori_loop(0, half, pair, 0)
        if count % 2:
            body(count - 1, 0)

    def tile(ref, i):
        return ref.at[i]

    def wait_send(ref, count, sem):
        part_of = ref.at[pl.ds(0, count)]
        remote(part_of, part_of, sem, sem, at_row(up_r)).wait_send()

    def wait_recv(ref, count, sem):
        part_of = ref.at[pl.ds(0, count)]
        remote(part_of, part_of, sem, sem, at_row(up_r)).wait_recv()

    sends_y, sends_z = (send_y0, send_y1, send_ym), (send_z0, send_z1, send_zm)

    def scatter_y(step):
        send_y = sends_y[step]

        def to_owner(i, _):
            j = lax.rem(me_r + i, lz)
            owner = owner_of(j)

            @pl.when(owner != me_r)
            def _():
                remote(
                    tile(send_y, j), tile(gat_y.at[step], me_r), sems.at[0, step], sems.at[1, step], at_row(owner)
                ).start()

            return 0

        lax.fori_loop(0, lz, to_owner, 0)

        @pl.when(owns)
        def _():
            gat_y[step, me_r] = send_y[me_owner_j]

    def scatter_z(step):
        send_z = sends_z[step]

        def to_owner(i, _):
            q = lax.rem(me_c + 1 + i, ncol)
            remote(
                tile(send_z, q), tile(gat_z.at[step], me_c), sems.at[2, step], sems.at[3, step], at_col(q)
            ).start()
            return 0

        for_each(ncol - 1, to_owner)
        gat_z[step, me_c] = send_z[me_c]

    def factor_owned(n, got, fac, mid):
        def read(r):
            return got[2, :, r, :]

        place = lax.broadcasted_iota(jnp.int32, (n, nx), 0)
        starts, ends = place == 0, place == n - 1
        beta = read(3)
        link = jnp.where(starts, 0.0, read(2))
        beta_up = jnp.where(ends, 0.0, roll(beta, n - 1, 0))
        link_up = jnp.where(ends, 0.0, roll(link, n - 1, 0))
        mid[0], mid[1], mid[2], mid[3] = beta, link, beta_up, link_up

        def keep(slot, values):
            fac[slot] = values

        excess = read(0) + jnp.where(ends, 1.0, roll(read(1), n - 1, 0))
        cyclic_setup(link, link_up, excess, 0, keep)

    def solve_owned(step, n, got, fac, mid, ret):
        def read(r):
            return got[step, :, r, :]

        place = lax.broadcasted_iota(jnp.int32, (n, nx), 0)
        starts, ends = place == 0, place == n - 1
        beta, link, beta_up, link_up = mid[0], mid[1], mid[2], mid[3]
        added = jnp.where(starts, 0.0, roll(read(2), 1, 0))
        phi = read(0) + link * added
        psi = read(1) + beta * added
        psi_up = jnp.where(ends, 0.0, roll(psi, n - 1, 0))
        last = cyclic_solve(phi + psi_up, 0, lambda slot: fac[slot])
        before = jnp.where(starts, 0.0, roll(last, 1, 0)) + added
        after = psi_up + beta_up * last + link_up * roll(last, n - 1, 0)
        ret[step, :, 0, :] = before
        ret[step, :, 1, :] = last
        ret[step, :, 2, :] = after

    def own_factors():
        wait_recv(gat_z.at[2], ncol - 1, sems.at[3, 2])
        factor_owned(ncol, gat_z, fac_z, mid_z)

        @pl.when(owns)
        def _():
            wait_recv(gat_y.at[2], nrow - 1, sems.at[1, 2])
            factor_owned(nrow, gat_y, fac_y, mid_y)

    def own_y(step):
        @pl.when(owns)
        def _():
            wait_recv(gat_y.at[step], nrow - 1, sems.at[1, step])
            solve_owned(step, nrow, gat_y, fac_y, mid_y, ret_y)

            def give(i, _):
                q = lax.rem(me_r + 1 + i, nrow)
                remote(
                    tile(ret_y.at[step], q), tile(res_y.at[step], me_owner_j), sems.at[4, step], sems.at[5, step], at_row(q)
                ).start()
                return 0

            for_each(nrow - 1, give)
            res_y[step, me_owner_j] = ret_y[step, me_r]

    def own_z(step):
        wait_recv(gat_z.at[step], ncol - 1, sems.at[3, step])
        solve_owned(step, ncol, gat_z, fac_z, mid_z, ret_z)

        def give(i, _):
            q = lax.rem(me_c + 1 + i, ncol)
            remote(
                tile(ret_z.at[step], q), tile(res_z.at[step], me_c), sems.at[6, step], sems.at[7, step], at_col(q)
            ).start()
            return 0

        for_each(ncol - 1, give)
        res_z[step, me_c] = ret_z[step, me_c]

    def wait_sent(step):
        send_y, send_z = sends_y[step], sends_z[step]

        @pl.when(owns)
        def _():
            wait_send(send_y, lz - 1, sems.at[0, step])
            if step < 2:
                wait_send(ret_y.at[step], nrow - 1, sems.at[4, step])

        @pl.when(others)
        def _():
            wait_send(send_y, lz, sems.at[0, step])

        wait_send(send_z, ncol - 1, sems.at[2, step])
        if step < 2:
            wait_send(ret_z.at[step], ncol - 1, sems.at[6, step])

    def wait_y(step):
        @pl.when(owns)
        def _():
            wait_recv(res_y.at[step], lz - 1, sems.at[5, step])

        @pl.when(others)
        def _():
            wait_recv(res_y.at[step], lz, sems.at[5, step])

    def wait_z(step):
        wait_recv(res_z.at[step], ncol - 1, sems.at[7, step])

    scatter_y(2)
    scatter_z(2)

    chunk = 32 if cells % 32 == 0 else 8

    def x_setup(c, _):
        at = pl.multiple_of(c * chunk, 8)
        excess = recip[pl.ds(at, chunk), :]
        lane = lax.broadcasted_iota(jnp.int32, excess.shape, 1)
        low = jnp.where(lane == 0, 0.0, 1.0)
        up = jnp.where(lane == nx - 1, 0.0, 1.0)

        def keep(slot, values):
            xfac[slot, pl.ds(at, chunk), :] = values

        cyclic_setup(low, up, excess + (1.0 - up), 1, keep)
        return 0

    lax.fori_loop(0, cells // chunk, x_setup, 0)

    lane = lax.broadcasted_iota(jnp.int32, (cells, nx), 1)

    def before_x(values):
        return jnp.where(lane == 0, 0.0, roll(values, 1, 1))

    def after_x(values):
        return jnp.where(lane == nx - 1, 0.0, roll(values, nx - 1, 1))

    def before_y(values, first, shifted):
        shifted[...] = roll(values, 1, 0)
        put_y(shifted, 0, first)
        return shifted[...]

    def after_y(values, last, shifted):
        shifted[...] = roll(values, cells - 1, 0)
        put_y(shifted, ly - 1, last)
        return shifted[...]

    def before_z(values, first):
        return jnp.concatenate([first, values[: cells - ly]], axis=0)

    def after_z(values, last):
        return jnp.concatenate([values[ly:], last], axis=0)

    def x_solve(f_ref, write):
        def lines(c, _):
            at = pl.multiple_of(c * chunk, 8)
            solved = cyclic_solve(
                f_ref[pl.ds(at, chunk), :], 1, lambda slot: xfac[slot, pl.ds(at, chunk), :]
            )
            column = lax.broadcasted_iota(jnp.int32, solved.shape, 1)
            ahead = jnp.where(column == nx - 1, 0.0, roll(solved, nx - 1, 1)) - solved
            write(pl.ds(at, chunk), solved, ahead)
            return 0

        lax.fori_loop(0, cells // chunk, lines, 0)

    zero_y = jnp.zeros((lz, nx), jnp.float32)
    zero_z = jnp.zeros((ly, nx), jnp.float32)

    mz_v = mz[...]
    ey_v = ey[...]
    ay_v = mz_v * inv_half - (after_x(ey_v) - ey_v)
    ay[...] = ay_v
    halos[0].wait_recv()
    my_v = my[...]
    my_before = before_z(my_v, halo_my[...] * gate_c)
    gx_v = keepf[...] * ex[...] - (my_v - my_before) * inv_half
    gx[...] = gx_v
    fx[...] = gx_v + (ay_v - before_y(ay_v, zero_y, sh0))
    rhs_forward(ly, row_y, fx, uy, ry, vy, send_y0, -row_y(ay, ly - 1))
    scatter_y(0)
    halos[1].wait_recv()
    ez_v = ez[...]
    mx_v = mx[...]
    ez_after = after_y(ez_v, halo_ez[pl.ds(0, lz), :] * gate_r_end, sh1)
    az_v = mx_v * inv_half - (ez_after - ez_v)
    az[...] = az_v
    gy_v = keepf[...] * ey_v - (mz_v - before_x(mz_v)) * inv_half
    gy[...] = gy_v
    fy[...] = gy_v + (az_v - before_z(az_v, zero_z))
    rhs_forward(lz, row_z, fy, uz, rz, vz, send_z0, -row_z(az, lz - 1))
    scatter_z(0)

    own_factors()
    halos[2].wait_recv()
    halos[3].wait_recv()
    ex_v = ex[...]
    ax_v = my[...] * inv_half - (after_z(ex_v, halo_ex[...] * gate_c_end) - ex_v)
    ax[...] = ax_v
    mx_v = mx[...]
    mx_before = before_y(mx_v, halo_mx[pl.ds(0, lz), :] * gate_r, sh2)
    gz_v = keepf[...] * ez[...] - (mx_v - mx_before) * inv_half
    gz[...] = gz_v
    fz[...] = gz_v + (ax_v - before_x(ax_v))

    def keep_half(at, solved, ahead):
        ez1[at, :] = solved
        dez[at, :] = ahead

    x_solve(fz, keep_half)
    cz_v = ax[...] + 2.0 * dez[...]
    cz[...] = cz_v
    fz[...] = twice[...] * ez1[...] - gz[...]
    fx[...] = (before_z(cz_v, zero_z) - cz_v) - gx[...]

    own_z(0)
    own_y(0)
    wait_z(0)
    back(lz, put_z, uz, rz, vz, res_z.at[0], ey1, dey)
    wait_y(0)
    back(ly, put_y, uy, ry, vy, res_y.at[0], ex1, dex)

    cx_v = ay[...] + 2.0 * dex[...]
    cy_v = az[...] + 2.0 * dey[...]
    cx[...], cy[...] = cx_v, cy_v
    fz[...] = fz[...] - (cy_v - before_y(cy_v, zero_y, sh1))
    fx[...] = fx[...] + twice[...] * ex1[...]

    rhs_forward(ly, row_y, fz, uy, ry, vy, send_y1, row_y(cy, ly - 1))
    scatter_y(1)
    rhs_forward(lz, row_z, fx, uz, rz, vz, send_z1, row_z(cz, lz - 1))
    scatter_z(1)

    cx_v = cx[...]
    fy[...] = (twice[...] * ey1[...] - gy[...]) - (cx_v - before_x(cx_v))

    def write_y(at, solved, ahead):
        ney[at, :] = solved
        nhz[at, :] = (cx[at, :] - ahead) * half_step

    x_solve(fy, write_y)
    store(1, 5)

    own_z(1)
    own_y(1)
    wait_z(1)
    back(lz, put_z, uz, rz, vz, res_z.at[1], nex, dez)
    nhy[...] = (cz[...] - dez[...]) * half_step
    store(0, 4)
    wait_y(1)
    back(ly, put_y, uy, ry, vy, res_y.at[1], nez, dex)
    nhx[...] = (cy[...] - dex[...]) * half_step
    store(2, 3)
    for step in range(3):
        wait_sent(step)
    for halo in halos:
        halo.wait_send()
    for done in stores:
        done.wait()


def deliver(*refs):
    made, placed, held = refs[:6], refs[6:12], refs[12:18]
    in_sem, out_sem = refs[18], refs[19]
    fetches = [
        pltpu.make_async_copy(made[i], held[i], in_sem.at[i]) for i in range(6)
    ]
    puts = [
        pltpu.make_async_copy(held[i], placed[i], out_sem.at[i]) for i in range(6)
    ]
    for fetch in fetches:
        fetch.start()
    for fetch, put in zip(fetches, puts):
        fetch.wait()
        put.start()
    for put in puts:
        put.wait()


def solution(mesh):
    nrow, ncol = mesh.shape["row"], mesh.shape["col"]

    def per_device(ex, ey, ez, mx, my, mz, tissue, permittivity, conductivity):
        lz, ly, nx = ex.shape
        cells, nt = lz * ly, permittivity.shape[0]
        f32 = jnp.float32
        flat = [a.reshape(cells, nx) for a in (ex, ey, ez, mx, my, mz, tissue)]
        whole = pltpu.VMEM((cells, nx), f32)
        pad_z = -(-lz // 8) * 8
        slots = lambda n: 2 * levels_of(n) + 1
        scratch = (
            [pltpu.SMEM((nt,), f32)] * 2
            + [whole] * 6
            + [pltpu.VMEM((cells, nx), jnp.int32)]
            + [whole] * 31
            + [pltpu.VMEM((slots(nx), cells, nx), f32)]
            + [pltpu.VMEM((ly - 1, lz, nx), f32)] * 3
            + [pltpu.VMEM((lz - 1, ly, nx), f32)] * 3
            + [pltpu.VMEM((lz, TILE, nx), f32)] * 3 + [pltpu.VMEM((ly, TILE, nx), f32)] * 3
            + [pltpu.VMEM((3, nrow, TILE, nx), f32), pltpu.VMEM((3, ncol, TILE, nx), f32)]
            + [pltpu.VMEM((2, nrow, TILE, nx), f32), pltpu.VMEM((2, ncol, TILE, nx), f32)]
            + [pltpu.VMEM((2, lz, TILE, nx), f32), pltpu.VMEM((2, ly, TILE, nx), f32)]
            + [pltpu.VMEM((slots(nrow), nrow, nx), f32), pltpu.VMEM((slots(ncol), ncol, nx), f32)]
            + [pltpu.VMEM((4, nrow, nx), f32), pltpu.VMEM((4, ncol, nx), f32)]
            + [pltpu.VMEM((pad_z, nx), f32)] * 4
            + [pltpu.VMEM((ly, nx), f32)] * 2
            + [
                pltpu.SemaphoreType.DMA((9,)),
                pltpu.SemaphoreType.DMA((6,)),
                pltpu.SemaphoreType.DMA((4,)),
                pltpu.SemaphoreType.DMA((4,)),
                pltpu.SemaphoreType.DMA((8, 3)),
            ]
        )
        outs = pl.pallas_call(
            functools.partial(kernel, (lz, ly, nx, nrow, ncol, nt)),
            out_shape=[jax.ShapeDtypeStruct((cells, nx), f32)] * 6,
            in_specs=[pl.BlockSpec(memory_space=pltpu.HBM)] * 9,
            out_specs=[pl.BlockSpec(memory_space=pltpu.HBM)] * 6,
            scratch_shapes=scratch,
            compiler_params=pltpu.CompilerParams(
                collective_id=0, has_side_effects=True, vmem_limit_bytes=VMEM_BYTES
            ),
        )(*flat, permittivity, conductivity)
        outs = pl.pallas_call(
            deliver,
            out_shape=[jax.ShapeDtypeStruct((cells, nx), f32)] * 6,
            in_specs=[pl.BlockSpec(memory_space=pltpu.HBM)] * 6,
            out_specs=[pl.BlockSpec(memory_space=pltpu.HBM)] * 6,
            scratch_shapes=[whole] * 6 + [pltpu.SemaphoreType.DMA((6,))] * 2,
            compiler_params=pltpu.CompilerParams(vmem_limit_bytes=VMEM_BYTES),
        )(*outs)
        return tuple(o.reshape(lz, ly, nx) for o in outs)

    cut = P("col", "row", None)
    return jax.shard_map(
        per_device,
        mesh=mesh,
        in_specs=(cut,) * 7 + (P(), P()),
        out_specs=(cut,) * 6,
        check_vma=False,
    )
```

```python
import functools

import jax
import jax.numpy as jnp
from jax import lax
from jax.experimental import pallas as pl
from jax.experimental.pallas import tpu as pltpu
from jax.sharding import PartitionSpec as P

MESH = pl.DeviceIdType.MESH
half_step = 32.0
inv_half = 1.0 / half_step
TILE = 4
VMEM_BYTES = 56 * 1024 * 1024


def roll(values, shift, axis):
    return pltpu.roll(values, shift, axis)


def cyclic_setup(low, up, excess, axis, keep):
    n = excess.shape[axis]
    stride = 1
    level = 0
    while stride < n:
        inv = 1.0 / (low + up + excess)
        from_low = low * roll(inv, stride, axis)
        from_up = up * roll(inv, n - stride, axis)
        excess = (
            excess
            + from_low * roll(excess, stride, axis)
            + from_up * roll(excess, n - stride, axis)
        )
        if 2 * stride < n:
            low = from_low * roll(low, stride, axis)
            up = from_up * roll(up, n - stride, axis)
        keep(2 * level, from_low)
        keep(2 * level + 1, from_up)
        stride, level = 2 * stride, level + 1
    keep(2 * level, 1.0 / excess)


def cyclic_solve(rhs, axis, kept):
    n = rhs.shape[axis]
    stride = 1
    level = 0
    while stride < n:
        rhs = (
            rhs
            + kept(2 * level) * roll(rhs, stride, axis)
            + kept(2 * level + 1) * roll(rhs, n - stride, axis)
        )
        stride, level = 2 * stride, level + 1
    return rhs * kept(2 * level)


def levels_of(n):
    return (n - 1).bit_length()


def kernel(sizes, *refs):
    lz, ly, nx, nrow, ncol, nt = sizes
    cells = lz * ly
    (ex_h, ey_h, ez_h, mx_h, my_h, mz_h, tis_h, eps_h, sig_h) = refs[:9]
    outs_h = refs[9:15]
    (
        eps_s, sig_s,
        ex, ey, ez, mx, my, mz, tis,
        nex, ney, nez, nhx, nhy, nhz,
        recip, keepf, twice, gx, gy, gz, ax, ay, az,
        fx, fy, fz, ex1, ey1, ez1, dex, dey, dez, cx, cy, cz,
        sh0, sh1, sh2, sh3,
        xfac,
        uy, ry, vy, uz, rz, vz,
        send_y0, send_y1, send_ym, send_z0, send_z1, send_zm, gat_y, gat_z, ret_y, ret_z, res_y, res_z,
        fac_y, fac_z, mid_y, mid_z,
        halo_mx_s, halo_ez_s, halo_mx, halo_ez, halo_my, halo_ex,
        load_sem, store_sem, halo_send, halo_recv, sems,
    ) = refs[15:]

    me_r, me_c = lax.axis_index("row"), lax.axis_index("col")
    gate_r = jnp.where(me_r > 0, 1.0, 0.0)
    gate_c = jnp.where(me_c > 0, 1.0, 0.0)
    gate_r_end = jnp.where(me_r < nrow - 1, 1.0, 0.0)
    gate_c_end = jnp.where(me_c < ncol - 1, 1.0, 0.0)

    def at_row(p):
        return (p, me_c)

    def at_col(p):
        return (me_r, p)

    loads = [
        pltpu.make_async_copy(src, dst, load_sem.at[i])
        for i, (src, dst) in enumerate(
            (
                (eps_h, eps_s),
                (sig_h, sig_s),
                (tis_h, tis),
                (mx_h, mx),
                (ez_h, ez),
                (my_h, my),
                (ex_h, ex),
                (ey_h, ey),
                (mz_h, mz),
            )
        )
    ]
    for load in loads:
        load.start()

    stores = [
        pltpu.make_async_copy(src, dst, store_sem.at[i])
        for i, (src, dst) in enumerate(zip((nex, ney, nez, nhx, nhy, nhz), outs_h))
    ]

    def store(*which):
        for i in which:
            stores[i].start()

    barrier = pltpu.get_barrier_semaphore()

    def greet_row(i, _):
        pl.semaphore_signal(
            barrier, inc=1, device_id=at_row(lax.rem(me_r + 1 + i, nrow)), device_id_type=MESH
        )
        return 0

    def greet_col(i, _):
        pl.semaphore_signal(
            barrier, inc=1, device_id=at_col(lax.rem(me_c + 1 + i, ncol)), device_id_type=MESH
        )
        return 0

    lax.fori_loop(0, nrow - 1, greet_row, 0)
    lax.fori_loop(0, ncol - 1, greet_col, 0)

    for load in loads[:3]:
        load.wait()
    part = cells // 2
    group = 4

    def look_up(c, _):
        at = pl.ds(pl.multiple_of(c * part, 8), part)
        label = tis[at, :]

        def tissues(g, carry):
            eps, sig = carry
            for j in range(group):
                t = g * group + j
                same = label == t
                eps = jnp.where(same, eps_s[t], eps)
                sig = jnp.where(same, sig_s[t], sig)
            return eps, sig

        zero = jnp.zeros(label.shape, jnp.float32)
        eps, sig = lax.fori_loop(0, nt // group, tissues, (zero, zero))
        loss = sig * (0.5 * half_step)
        scale = inv_half * inv_half
        recip[at, :] = (eps + loss) * scale
        keepf[at, :] = (eps - loss) * scale
        twice[at, :] = eps * (2.0 * scale)
        return 0

    lax.fori_loop(0, 2, look_up, 0)

    for load in loads[3:]:
        load.wait()

    def row_y(ref, i):
        return ref[pl.ds(i, lz, stride=ly), :]

    def put_y(ref, i, values):
        ref[pl.ds(i, lz, stride=ly), :] = values

    def row_z(ref, i):
        return ref[pl.ds(i * ly, ly), :]

    def put_z(ref, i, values):
        ref[pl.ds(i * ly, ly), :] = values

    def matrix_forward(n, row, gate, u_ref, r_ref, send):
        share = row(recip, 0)
        rest = share + gate
        inv = 1.0 / (1.0 + rest)
        reach = inv
        gain = share * inv
        beta, gains = reach, gain
        u_ref[0], r_ref[0] = reach, inv
        for i in range(1, n - 1):
            share = row(recip, i)
            rest = share + rest * inv
            inv = 1.0 / (1.0 + rest)
            gain = (share + gain) * inv
            gains = gains + reach * gain
            further = reach * inv
            beta = beta + reach * further
            reach = further
            u_ref[i], r_ref[i] = reach, inv
        send[:, 0, :] = row(recip, n - 1) + gain
        send[:, 1, :] = gains
        send[:, 2, :] = reach
        send[:, 3, :] = beta

    matrix_forward(ly, row_y, gate_r, uy, ry, send_ym)
    matrix_forward(lz, row_z, gate_c, uz, rz, send_zm)

    halo_mx_s[pl.ds(0, lz), :] = row_y(mx, ly - 1)
    halo_ez_s[pl.ds(0, lz), :] = row_y(ez, 0)
    pl.semaphore_wait(barrier, nrow + ncol - 2)

    up_r, down_r = lax.rem(me_r + 1, nrow), lax.rem(me_r + nrow - 1, nrow)
    up_c, down_c = lax.rem(me_c + 1, ncol), lax.rem(me_c + ncol - 1, ncol)

    def remote(src, dst, send_sem, recv_sem, device):
        return pltpu.make_async_remote_copy(
            src_ref=src,
            dst_ref=dst,
            send_sem=send_sem,
            recv_sem=recv_sem,
            device_id=device,
            device_id_type=MESH,
        )

    halos = [
        remote(my.at[pl.ds(cells - ly, ly), :], halo_my, halo_send.at[0], halo_recv.at[0], at_col(up_c)),
        remote(halo_ez_s, halo_ez, halo_send.at[1], halo_recv.at[1], at_row(down_r)),
        remote(halo_mx_s, halo_mx, halo_send.at[2], halo_recv.at[2], at_row(up_r)),
        remote(ex.at[pl.ds(0, ly), :], halo_ex, halo_send.at[3], halo_recv.at[3], at_col(down_c)),
    ]
    for halo in halos:
        halo.start()

    def rhs_forward(n, row, f_ref, u_ref, r_ref, v_ref, send, passed_on):
        value = row(f_ref, 0) * r_ref[0]
        psi = value
        v_ref[0] = value
        for i in range(1, n - 1):
            value = (row(f_ref, i) + value) * r_ref[i]
            psi = psi + u_ref[i - 1] * value
            v_ref[i] = value
        send[:, 0, :] = row(f_ref, n - 1) + value
        send[:, 1, :] = psi
        send[:, 2, :] = passed_on

    def back(n, row_put, u_ref, r_ref, v_ref, got, out, diff):
        before = got[:, 0, :]
        value = got[:, 1, :]
        row_put(out, n - 1, value)
        row_put(diff, n - 1, got[:, 2, :] - value)
        for i in range(n - 2, -1, -1):
            lower = (v_ref[i] + u_ref[i] * before) + r_ref[i] * value
            row_put(out, i, lower)
            row_put(diff, i, value - lower)
            value = lower


    me_owner_j = lax.div(lz * me_r + nrow - 1, nrow)

    def owner_of(j):
        return lax.div(j * nrow, lz)

    owns = jnp.logical_and(me_owner_j < lz, owner_of(me_owner_j) == me_r)
    others = jnp.logical_not(owns)

    def for_each(count, body):
        half = count // 2

        def pair(k, _):
            body(half + k, 0)
            body(half - 1 - k, 0)
            return 0

        lax.fori_loop(0, half, pair, 0)
        if count % 2:
            body(count - 1, 0)

    def tile(ref, i):
        return ref.at[i]

    def wait_send(ref, count, sem):
        part_of = ref.at[pl.ds(0, count)]
        remote(part_of, part_of, sem, sem, at_row(up_r)).wait_send()

    def wait_recv(ref, count, sem):
        part_of = ref.at[pl.ds(0, count)]
        remote(part_of, part_of, sem, sem, at_row(up_r)).wait_recv()

    sends_y, sends_z = (send_y0, send_y1, send_ym), (send_z0, send_z1, send_zm)

    def scatter_y(step):
        send_y = sends_y[step]

        def to_owner(i, _):
            j = lax.rem(me_r + i, lz)
            owner = owner_of(j)

            @pl.when(owner != me_r)
            def _():
                remote(
                    tile(send_y, j), tile(gat_y.at[step], me_r), sems.at[0, step], sems.at[1, step], at_row(owner)
                ).start()

            return 0

        lax.fori_loop(0, lz, to_owner, 0)

        @pl.when(owns)
        def _():
            gat_y[step, me_r] = send_y[me_owner_j]

    def scatter_z(step):
        send_z = sends_z[step]

        def to_owner(i, _):
            q = lax.rem(me_c + 1 + i, ncol)
            remote(
                tile(send_z, q), tile(gat_z.at[step], me_c), sems.at[2, step], sems.at[3, step], at_col(q)
            ).start()
            return 0

        for_each(ncol - 1, to_owner)
        gat_z[step, me_c] = send_z[me_c]

    def factor_owned(n, got, fac, mid):
        def read(r):
            return got[2, :, r, :]

        place = lax.broadcasted_iota(jnp.int32, (n, nx), 0)
        starts, ends = place == 0, place == n - 1
        beta = read(3)
        link = jnp.where(starts, 0.0, read(2))
        beta_up = jnp.where(ends, 0.0, roll(beta, n - 1, 0))
        link_up = jnp.where(ends, 0.0, roll(link, n - 1, 0))
        mid[0], mid[1], mid[2], mid[3] = beta, link, beta_up, link_up

        def keep(slot, values):
            fac[slot] = values

        excess = read(0) + jnp.where(ends, 1.0, roll(read(1), n - 1, 0))
        cyclic_setup(link, link_up, excess, 0, keep)

    def solve_owned(step, n, got, fac, mid, ret):
        def read(r):
            return got[step, :, r, :]

        place = lax.broadcasted_iota(jnp.int32, (n, nx), 0)
        starts, ends = place == 0, place == n - 1
        beta, link, beta_up, link_up = mid[0], mid[1], mid[2], mid[3]
        added = jnp.where(starts, 0.0, roll(read(2), 1, 0))
        phi = read(0) + link * added
        psi = read(1) + beta * added
        psi_up = jnp.where(ends, 0.0, roll(psi, n - 1, 0))
        last = cyclic_solve(phi + psi_up, 0, lambda slot: fac[slot])
        before = jnp.where(starts, 0.0, roll(last, 1, 0)) + added
        after = psi_up + beta_up * last + link_up * roll(last, n - 1, 0)
        ret[step, :, 0, :] = before
        ret[step, :, 1, :] = last
        ret[step, :, 2, :] = after

    def own_factors():
        wait_recv(gat_z.at[2], ncol - 1, sems.at[3, 2])
        factor_owned(ncol, gat_z, fac_z, mid_z)

        @pl.when(owns)
        def _():
            wait_recv(gat_y.at[2], nrow - 1, sems.at[1, 2])
            factor_owned(nrow, gat_y, fac_y, mid_y)

    def own_y(step):
        @pl.when(owns)
        def _():
            wait_recv(gat_y.at[step], nrow - 1, sems.at[1, step])
            solve_owned(step, nrow, gat_y, fac_y, mid_y, ret_y)

            def give(i, _):
                q = lax.rem(me_r + 1 + i, nrow)
                remote(
                    tile(ret_y.at[step], q), tile(res_y.at[step], me_owner_j), sems.at[4, step], sems.at[5, step], at_row(q)
                ).start()
                return 0

            for_each(nrow - 1, give)
            res_y[step, me_owner_j] = ret_y[step, me_r]

    def own_z(step):
        wait_recv(gat_z.at[step], ncol - 1, sems.at[3, step])
        solve_owned(step, ncol, gat_z, fac_z, mid_z, ret_z)

        def give(i, _):
            q = lax.rem(me_c + 1 + i, ncol)
            remote(
                tile(ret_z.at[step], q), tile(res_z.at[step], me_c), sems.at[6, step], sems.at[7, step], at_col(q)
            ).start()
            return 0

        for_each(ncol - 1, give)
        res_z[step, me_c] = ret_z[step, me_c]

    def wait_sent(step):
        send_y, send_z = sends_y[step], sends_z[step]

        @pl.when(owns)
        def _():
            wait_send(send_y, lz - 1, sems.at[0, step])
            if step < 2:
                wait_send(ret_y.at[step], nrow - 1, sems.at[4, step])

        @pl.when(others)
        def _():
            wait_send(send_y, lz, sems.at[0, step])

        wait_send(send_z, ncol - 1, sems.at[2, step])
        if step < 2:
            wait_send(ret_z.at[step], ncol - 1, sems.at[6, step])

    def wait_y(step):
        @pl.when(owns)
        def _():
            wait_recv(res_y.at[step], lz - 1, sems.at[5, step])

        @pl.when(others)
        def _():
            wait_recv(res_y.at[step], lz, sems.at[5, step])

    def wait_z(step):
        wait_recv(res_z.at[step], ncol - 1, sems.at[7, step])

    scatter_y(2)
    scatter_z(2)

    chunk = 96 if cells % 96 == 0 else 8

    def x_setup(c, _):
        at = pl.multiple_of(c * chunk, 8)
        excess = recip[pl.ds(at, chunk), :]
        lane = lax.broadcasted_iota(jnp.int32, excess.shape, 1)
        low = jnp.where(lane == 0, 0.0, 1.0)
        up = jnp.where(lane == nx - 1, 0.0, 1.0)

        def keep(slot, values):
            xfac[slot, pl.ds(at, chunk), :] = values

        cyclic_setup(low, up, excess + (1.0 - up), 1, keep)
        return 0

    lax.fori_loop(0, cells // chunk, x_setup, 0)

    lane = lax.broadcasted_iota(jnp.int32, (cells, nx), 1)

    def before_x(values):
        return jnp.where(lane == 0, 0.0, roll(values, 1, 1))

    def after_x(values):
        return jnp.where(lane == nx - 1, 0.0, roll(values, nx - 1, 1))

    def before_y(values, first, shifted):
        shifted[...] = roll(values, 1, 0)
        put_y(shifted, 0, first)
        return shifted[...]

    def after_y(values, last, shifted):
        shifted[...] = roll(values, cells - 1, 0)
        put_y(shifted, ly - 1, last)
        return shifted[...]

    def before_z(values, first):
        return jnp.concatenate([first, values[: cells - ly]], axis=0)

    def after_z(values, last):
        return jnp.concatenate([values[ly:], last], axis=0)

    def x_solve(f_ref, write):
        def lines(c, _):
            at = pl.multiple_of(c * chunk, 8)
            solved = cyclic_solve(
                f_ref[pl.ds(at, chunk), :], 1, lambda slot: xfac[slot, pl.ds(at, chunk), :]
            )
            column = lax.broadcasted_iota(jnp.int32, solved.shape, 1)
            ahead = jnp.where(column == nx - 1, 0.0, roll(solved, nx - 1, 1)) - solved
            write(pl.ds(at, chunk), solved, ahead)
            return 0

        lax.fori_loop(0, cells // chunk, lines, 0)

    zero_y = jnp.zeros((lz, nx), jnp.float32)
    zero_z = jnp.zeros((ly, nx), jnp.float32)

    mz_v = mz[...]
    ey_v = ey[...]
    ay_v = mz_v * inv_half - (after_x(ey_v) - ey_v)
    ay[...] = ay_v
    halos[0].wait_recv()
    my_v = my[...]
    my_before = before_z(my_v, halo_my[...] * gate_c)
    gx_v = keepf[...] * ex[...] - (my_v - my_before) * inv_half
    gx[...] = gx_v
    fx[...] = gx_v + (ay_v - before_y(ay_v, zero_y, sh0))
    rhs_forward(ly, row_y, fx, uy, ry, vy, send_y0, -row_y(ay, ly - 1))
    scatter_y(0)
    halos[1].wait_recv()
    ez_v = ez[...]
    mx_v = mx[...]
    ez_after = after_y(ez_v, halo_ez[pl.ds(0, lz), :] * gate_r_end, sh1)
    az_v = mx_v * inv_half - (ez_after - ez_v)
    az[...] = az_v
    gy_v = keepf[...] * ey_v - (mz_v - before_x(mz_v)) * inv_half
    gy[...] = gy_v
    fy[...] = gy_v + (az_v - before_z(az_v, zero_z))
    rhs_forward(lz, row_z, fy, uz, rz, vz, send_z0, -row_z(az, lz - 1))
    scatter_z(0)

    own_factors()
    halos[2].wait_recv()
    halos[3].wait_recv()
    ex_v = ex[...]
    ax_v = my[...] * inv_half - (after_z(ex_v, halo_ex[...] * gate_c_end) - ex_v)
    ax[...] = ax_v
    mx_v = mx[...]
    mx_before = before_y(mx_v, halo_mx[pl.ds(0, lz), :] * gate_r, sh2)
    gz_v = keepf[...] * ez[...] - (mx_v - mx_before) * inv_half
    gz[...] = gz_v
    fz[...] = gz_v + (ax_v - before_x(ax_v))

    def keep_half(at, solved, ahead):
        ez1[at, :] = solved
        dez[at, :] = ahead

    x_solve(fz, keep_half)
    cz_v = ax[...] + 2.0 * dez[...]
    cz[...] = cz_v
    fz[...] = twice[...] * ez1[...] - gz[...]
    fx[...] = (before_z(cz_v, zero_z) - cz_v) - gx[...]

    own_y(0)
    own_z(0)
    wait_z(0)
    back(lz, put_z, uz, rz, vz, res_z.at[0], ey1, dey)
    wait_y(0)
    back(ly, put_y, uy, ry, vy, res_y.at[0], ex1, dex)

    cx_v = ay[...] + 2.0 * dex[...]
    cy_v = az[...] + 2.0 * dey[...]
    cx[...], cy[...] = cx_v, cy_v
    fz[...] = fz[...] - (cy_v - before_y(cy_v, zero_y, sh1))
    fx[...] = fx[...] + twice[...] * ex1[...]

    rhs_forward(ly, row_y, fz, uy, ry, vy, send_y1, row_y(cy, ly - 1))
    scatter_y(1)
    rhs_forward(lz, row_z, fx, uz, rz, vz, send_z1, row_z(cz, lz - 1))
    scatter_z(1)

    cx_v = cx[...]
    fy[...] = (twice[...] * ey1[...] - gy[...]) - (cx_v - before_x(cx_v))

    def write_y(at, solved, ahead):
        ney[at, :] = solved
        nhz[at, :] = (cx[at, :] - ahead) * half_step

    x_solve(fy, write_y)
    store(1, 5)

    own_y(1)
    own_z(1)
    wait_z(1)
    back(lz, put_z, uz, rz, vz, res_z.at[1], nex, dez)
    nhy[...] = (cz[...] - dez[...]) * half_step
    store(0, 4)
    wait_y(1)
    back(ly, put_y, uy, ry, vy, res_y.at[1], nez, dex)
    nhx[...] = (cy[...] - dex[...]) * half_step
    store(2, 3)
    for step in range(3):
        wait_sent(step)
    for halo in halos:
        halo.wait_send()
    for done in stores:
        done.wait()


def deliver(*refs):
    made, placed, held = refs[:6], refs[6:12], refs[12:18]
    in_sem, out_sem = refs[18], refs[19]
    fetches = [
        pltpu.make_async_copy(made[i], held[i], in_sem.at[i]) for i in range(6)
    ]
    puts = [
        pltpu.make_async_copy(held[i], placed[i], out_sem.at[i]) for i in range(6)
    ]
    for fetch in fetches:
        fetch.start()
    for fetch, put in zip(fetches, puts):
        fetch.wait()
        put.start()
    for put in puts:
        put.wait()


def solution(mesh):
    nrow, ncol = mesh.shape["row"], mesh.shape["col"]

    def per_device(ex, ey, ez, mx, my, mz, tissue, permittivity, conductivity):
        lz, ly, nx = ex.shape
        cells, nt = lz * ly, permittivity.shape[0]
        f32 = jnp.float32
        flat = [a.reshape(cells, nx) for a in (ex, ey, ez, mx, my, mz, tissue)]
        whole = pltpu.VMEM((cells, nx), f32)
        pad_z = -(-lz // 8) * 8
        slots = lambda n: 2 * levels_of(n) + 1
        scratch = (
            [pltpu.SMEM((nt,), f32)] * 2
            + [whole] * 6
            + [pltpu.VMEM((cells, nx), jnp.int32)]
            + [whole] * 31
            + [pltpu.VMEM((slots(nx), cells, nx), f32)]
            + [pltpu.VMEM((ly - 1, lz, nx), f32)] * 3
            + [pltpu.VMEM((lz - 1, ly, nx), f32)] * 3
            + [pltpu.VMEM((lz, TILE, nx), f32)] * 3 + [pltpu.VMEM((ly, TILE, nx), f32)] * 3
            + [pltpu.VMEM((3, nrow, TILE, nx), f32), pltpu.VMEM((3, ncol, TILE, nx), f32)]
            + [pltpu.VMEM((2, nrow, TILE, nx), f32), pltpu.VMEM((2, ncol, TILE, nx), f32)]
            + [pltpu.VMEM((2, lz, TILE, nx), f32), pltpu.VMEM((2, ly, TILE, nx), f32)]
            + [pltpu.VMEM((slots(nrow), nrow, nx), f32), pltpu.VMEM((slots(ncol), ncol, nx), f32)]
            + [pltpu.VMEM((4, nrow, nx), f32), pltpu.VMEM((4, ncol, nx), f32)]
            + [pltpu.VMEM((pad_z, nx), f32)] * 4
            + [pltpu.VMEM((ly, nx), f32)] * 2
            + [
                pltpu.SemaphoreType.DMA((9,)),
                pltpu.SemaphoreType.DMA((6,)),
                pltpu.SemaphoreType.DMA((4,)),
                pltpu.SemaphoreType.DMA((4,)),
                pltpu.SemaphoreType.DMA((8, 3)),
            ]
        )
        outs = pl.pallas_call(
            functools.partial(kernel, (lz, ly, nx, nrow, ncol, nt)),
            out_shape=[jax.ShapeDtypeStruct((cells, nx), f32)] * 6,
            in_specs=[pl.BlockSpec(memory_space=pltpu.HBM)] * 9,
            out_specs=[pl.BlockSpec(memory_space=pltpu.HBM)] * 6,
            scratch_shapes=scratch,
            compiler_params=pltpu.CompilerParams(
                collective_id=0, has_side_effects=True, vmem_limit_bytes=VMEM_BYTES
            ),
        )(*flat, permittivity, conductivity)
        outs = pl.pallas_call(
            deliver,
            out_shape=[jax.ShapeDtypeStruct((cells, nx), f32)] * 6,
            in_specs=[pl.BlockSpec(memory_space=pltpu.HBM)] * 6,
            out_specs=[pl.BlockSpec(memory_space=pltpu.HBM)] * 6,
            scratch_shapes=[whole] * 6 + [pltpu.SemaphoreType.DMA((6,))] * 2,
            compiler_params=pltpu.CompilerParams(vmem_limit_bytes=VMEM_BYTES),
        )(*outs)
        return tuple(o.reshape(lz, ly, nx) for o in outs)

    cut = P("col", "row", None)
    return jax.shard_map(
        per_device,
        mesh=mesh,
        in_specs=(cut,) * 7 + (P(), P()),
        out_specs=(cut,) * 6,
        check_vma=False,
    )
```

```python
import functools

import jax
import jax.numpy as jnp
from jax import lax
from jax.experimental import pallas as pl
from jax.experimental.pallas import tpu as pltpu
from jax.sharding import PartitionSpec as P

MESH = pl.DeviceIdType.MESH
half_step = 32.0
inv_half = 1.0 / half_step
TILE = 4
VMEM_BYTES = 56 * 1024 * 1024


def roll(values, shift, axis):
    return pltpu.roll(values, shift, axis)


def cyclic_setup(low, up, excess, axis, keep):
    n = excess.shape[axis]
    stride = 1
    level = 0
    while stride < n:
        inv = 1.0 / (low + up + excess)
        from_low = low * roll(inv, stride, axis)
        from_up = up * roll(inv, n - stride, axis)
        excess = (
            excess
            + from_low * roll(excess, stride, axis)
            + from_up * roll(excess, n - stride, axis)
        )
        if 2 * stride < n:
            low = from_low * roll(low, stride, axis)
            up = from_up * roll(up, n - stride, axis)
        keep(2 * level, from_low)
        keep(2 * level + 1, from_up)
        stride, level = 2 * stride, level + 1
    keep(2 * level, 1.0 / excess)


def cyclic_solve(rhs, axis, kept):
    n = rhs.shape[axis]
    stride = 1
    level = 0
    while stride < n:
        rhs = (
            rhs
            + kept(2 * level) * roll(rhs, stride, axis)
            + kept(2 * level + 1) * roll(rhs, n - stride, axis)
        )
        stride, level = 2 * stride, level + 1
    return rhs * kept(2 * level)


def levels_of(n):
    return (n - 1).bit_length()


def kernel(sizes, *refs):
    lz, ly, nx, nrow, ncol, nt = sizes
    cells = lz * ly
    (ex_h, ey_h, ez_h, mx_h, my_h, mz_h, tis_h, eps_h, sig_h) = refs[:9]
    outs_h = refs[9:15]
    (
        eps_s, sig_s,
        ex, ey, ez, mx, my, mz, tis,
        nex, ney, nez, nhx, nhy, nhz,
        recip, keepf, twice, gx, gy, gz, ax, ay, az,
        fx, fy, fz, ex1, ey1, ez1, dex, dey, dez, cx, cy, cz,
        sh0, sh1, sh2, sh3,
        xfac,
        uy, ry, vy, wy, uz, rz, vz,
        send_y0, send_y1, send_ym, send_z0, send_z1, send_zm, gat_y, gat_z, ret_y, ret_z, res_y, res_z,
        fac_y, fac_z, mid_y, mid_z,
        halo_mx_s, halo_ez_s, halo_mx, halo_ez, halo_my, halo_ex,
        load_sem, store_sem, halo_send, halo_recv, sems,
    ) = refs[15:]

    me_r, me_c = lax.axis_index("row"), lax.axis_index("col")
    gate_r = jnp.where(me_r > 0, 1.0, 0.0)
    gate_c = jnp.where(me_c > 0, 1.0, 0.0)
    gate_r_end = jnp.where(me_r < nrow - 1, 1.0, 0.0)
    gate_c_end = jnp.where(me_c < ncol - 1, 1.0, 0.0)

    def at_row(p):
        return (p, me_c)

    def at_col(p):
        return (me_r, p)

    loads = [
        pltpu.make_async_copy(src, dst, load_sem.at[i])
        for i, (src, dst) in enumerate(
            (
                (eps_h, eps_s),
                (sig_h, sig_s),
                (tis_h, tis),
                (mx_h, mx),
                (ez_h, ez),
                (my_h, my),
                (ex_h, ex),
                (ey_h, ey),
                (mz_h, mz),
            )
        )
    ]
    for load in loads:
        load.start()

    stores = [
        pltpu.make_async_copy(src, dst, store_sem.at[i])
        for i, (src, dst) in enumerate(zip((nex, ney, nez, nhx, nhy, nhz), outs_h))
    ]

    def store(*which):
        for i in which:
            stores[i].start()

    barrier = pltpu.get_barrier_semaphore()

    def greet_row(i, _):
        pl.semaphore_signal(
            barrier, inc=1, device_id=at_row(lax.rem(me_r + 1 + i, nrow)), device_id_type=MESH
        )
        return 0

    def greet_col(i, _):
        pl.semaphore_signal(
            barrier, inc=1, device_id=at_col(lax.rem(me_c + 1 + i, ncol)), device_id_type=MESH
        )
        return 0

    lax.fori_loop(0, nrow - 1, greet_row, 0)
    lax.fori_loop(0, ncol - 1, greet_col, 0)

    for load in loads[:3]:
        load.wait()
    part = cells // 2
    group = 4

    def look_up(c, _):
        at = pl.ds(pl.multiple_of(c * part, 8), part)
        label = tis[at, :]

        def tissues(g, carry):
            eps, sig = carry
            for j in range(group):
                t = g * group + j
                same = label == t
                eps = jnp.where(same, eps_s[t], eps)
                sig = jnp.where(same, sig_s[t], sig)
            return eps, sig

        zero = jnp.zeros(label.shape, jnp.float32)
        eps, sig = lax.fori_loop(0, nt // group, tissues, (zero, zero))
        loss = sig * (0.5 * half_step)
        scale = inv_half * inv_half
        recip[at, :] = (eps + loss) * scale
        keepf[at, :] = (eps - loss) * scale
        twice[at, :] = eps * (2.0 * scale)
        return 0

    lax.fori_loop(0, 2, look_up, 0)

    for load in loads[3:]:
        load.wait()

    def row_y(ref, i):
        return ref[pl.ds(i, lz, stride=ly), :]

    def put_y(ref, i, values):
        ref[pl.ds(i, lz, stride=ly), :] = values

    def row_z(ref, i):
        return ref[pl.ds(i * ly, ly), :]

    def put_z(ref, i, values):
        ref[pl.ds(i * ly, ly), :] = values

    def matrix_forward(n, row, gate, u_ref, r_ref, send):
        share = row(recip, 0)
        rest = share + gate
        inv = 1.0 / (1.0 + rest)
        reach = inv
        gain = share * inv
        beta, gains = reach, gain
        u_ref[0], r_ref[0] = reach, inv
        for i in range(1, n - 1):
            share = row(recip, i)
            rest = share + rest * inv
            inv = 1.0 / (1.0 + rest)
            gain = (share + gain) * inv
            gains = gains + reach * gain
            further = reach * inv
            beta = beta + reach * further
            reach = further
            u_ref[i], r_ref[i] = reach, inv
        send[:, 0, :] = row(recip, n - 1) + gain
        send[:, 1, :] = gains
        send[:, 2, :] = reach
        send[:, 3, :] = beta

    matrix_forward(ly, row_y, gate_r, uy, ry, send_ym)
    matrix_forward(lz, row_z, gate_c, uz, rz, send_zm)

    halo_mx_s[pl.ds(0, lz), :] = row_y(mx, ly - 1)
    halo_ez_s[pl.ds(0, lz), :] = row_y(ez, 0)
    pl.semaphore_wait(barrier, nrow + ncol - 2)

    up_r, down_r = lax.rem(me_r + 1, nrow), lax.rem(me_r + nrow - 1, nrow)
    up_c, down_c = lax.rem(me_c + 1, ncol), lax.rem(me_c + ncol - 1, ncol)

    def remote(src, dst, send_sem, recv_sem, device):
        return pltpu.make_async_remote_copy(
            src_ref=src,
            dst_ref=dst,
            send_sem=send_sem,
            recv_sem=recv_sem,
            device_id=device,
            device_id_type=MESH,
        )

    halos = [
        remote(my.at[pl.ds(cells - ly, ly), :], halo_my, halo_send.at[0], halo_recv.at[0], at_col(up_c)),
        remote(halo_ez_s, halo_ez, halo_send.at[1], halo_recv.at[1], at_row(down_r)),
        remote(halo_mx_s, halo_mx, halo_send.at[2], halo_recv.at[2], at_row(up_r)),
        remote(ex.at[pl.ds(0, ly), :], halo_ex, halo_send.at[3], halo_recv.at[3], at_col(down_c)),
    ]
    for halo in halos:
        halo.start()

    def rhs_forward(n, row, f_ref, u_ref, r_ref, v_ref, send, passed_on):
        value = row(f_ref, 0) * r_ref[0]
        psi = value
        v_ref[0] = value
        for i in range(1, n - 1):
            value = (row(f_ref, i) + value) * r_ref[i]
            psi = psi + u_ref[i - 1] * value
            v_ref[i] = value
        send[:, 0, :] = row(f_ref, n - 1) + value
        send[:, 1, :] = psi
        send[:, 2, :] = passed_on

    def back(n, row_put, u_ref, r_ref, v_ref, got, out, diff):
        before = got[:, 0, :]
        value = got[:, 1, :]
        row_put(out, n - 1, value)
        row_put(diff, n - 1, got[:, 2, :] - value)
        for i in range(n - 2, -1, -1):
            lower = (v_ref[i] + u_ref[i] * before) + r_ref[i] * value
            row_put(out, i, lower)
            row_put(diff, i, value - lower)
            value = lower


    me_owner_j = lax.div(lz * me_r + nrow - 1, nrow)

    def owner_of(j):
        return lax.div(j * nrow, lz)

    owns = jnp.logical_and(me_owner_j < lz, owner_of(me_owner_j) == me_r)
    others = jnp.logical_not(owns)

    def for_each(count, body):
        half = count // 2

        def pair(k, _):
            body(half + k, 0)
            body(half - 1 - k, 0)
            return 0

        lax.fori_loop(0, half, pair, 0)
        if count % 2:
            body(count - 1, 0)

    def tile(ref, i):
        return ref.at[i]

    def wait_send(ref, count, sem):
        part_of = ref.at[pl.ds(0, count)]
        remote(part_of, part_of, sem, sem, at_row(up_r)).wait_send()

    def wait_recv(ref, count, sem):
        part_of = ref.at[pl.ds(0, count)]
        remote(part_of, part_of, sem, sem, at_row(up_r)).wait_recv()

    sends_y, sends_z = (send_y0, send_y1, send_ym), (send_z0, send_z1, send_zm)

    def scatter_y(step):
        send_y = sends_y[step]

        def to_owner(i, _):
            j = lax.rem(me_r + i, lz)
            owner = owner_of(j)

            @pl.when(owner != me_r)
            def _():
                remote(
                    tile(send_y, j), tile(gat_y.at[step], me_r), sems.at[0, step], sems.at[1, step], at_row(owner)
                ).start()

            return 0

        lax.fori_loop(0, lz, to_owner, 0)

        @pl.when(owns)
        def _():
            gat_y[step, me_r] = send_y[me_owner_j]

    def scatter_z(step):
        send_z = sends_z[step]

        def to_owner(i, _):
            q = lax.rem(me_c + 1 + i, ncol)
            remote(
                tile(send_z, q), tile(gat_z.at[step], me_c), sems.at[2, step], sems.at[3, step], at_col(q)
            ).start()
            return 0

        for_each(ncol - 1, to_owner)
        gat_z[step, me_c] = send_z[me_c]

    def factor_owned(n, got, fac, mid):
        def read(r):
            return got[2, :, r, :]

        place = lax.broadcasted_iota(jnp.int32, (n, nx), 0)
        starts, ends = place == 0, place == n - 1
        beta = read(3)
        link = jnp.where(starts, 0.0, read(2))
        beta_up = jnp.where(ends, 0.0, roll(beta, n - 1, 0))
        link_up = jnp.where(ends, 0.0, roll(link, n - 1, 0))
        mid[0], mid[1], mid[2], mid[3] = beta, link, beta_up, link_up

        def keep(slot, values):
            fac[slot] = values

        excess = read(0) + jnp.where(ends, 1.0, roll(read(1), n - 1, 0))
        cyclic_setup(link, link_up, excess, 0, keep)

    def solve_owned(step, n, got, fac, mid, ret):
        def read(r):
            return got[step, :, r, :]

        place = lax.broadcasted_iota(jnp.int32, (n, nx), 0)
        starts, ends = place == 0, place == n - 1
        beta, link, beta_up, link_up = mid[0], mid[1], mid[2], mid[3]
        added = jnp.where(starts, 0.0, roll(read(2), 1, 0))
        phi = read(0) + link * added
        psi = read(1) + beta * added
        psi_up = jnp.where(ends, 0.0, roll(psi, n - 1, 0))
        last = cyclic_solve(phi + psi_up, 0, lambda slot: fac[slot])
        before = jnp.where(starts, 0.0, roll(last, 1, 0)) + added
        after = psi_up + beta_up * last + link_up * roll(last, n - 1, 0)
        ret[step, :, 0, :] = before
        ret[step, :, 1, :] = last
        ret[step, :, 2, :] = after

    def own_factors():
        wait_recv(gat_z.at[2], ncol - 1, sems.at[3, 2])
        factor_owned(ncol, gat_z, fac_z, mid_z)

        @pl.when(owns)
        def _():
            wait_recv(gat_y.at[2], nrow - 1, sems.at[1, 2])
            factor_owned(nrow, gat_y, fac_y, mid_y)

    def own_y(step):
        @pl.when(owns)
        def _():
            wait_recv(gat_y.at[step], nrow - 1, sems.at[1, step])
            solve_owned(step, nrow, gat_y, fac_y, mid_y, ret_y)

            def give(i, _):
                q = lax.rem(me_r + 1 + i, nrow)
                remote(
                    tile(ret_y.at[step], q), tile(res_y.at[step], me_owner_j), sems.at[4, step], sems.at[5, step], at_row(q)
                ).start()
                return 0

            for_each(nrow - 1, give)
            res_y[step, me_owner_j] = ret_y[step, me_r]

    def own_z(step):
        wait_recv(gat_z.at[step], ncol - 1, sems.at[3, step])
        solve_owned(step, ncol, gat_z, fac_z, mid_z, ret_z)

        def give(i, _):
            q = lax.rem(me_c + 1 + i, ncol)
            remote(
                tile(ret_z.at[step], q), tile(res_z.at[step], me_c), sems.at[6, step], sems.at[7, step], at_col(q)
            ).start()
            return 0

        for_each(ncol - 1, give)
        res_z[step, me_c] = ret_z[step, me_c]

    def wait_sent(step):
        send_y, send_z = sends_y[step], sends_z[step]

        @pl.when(owns)
        def _():
            wait_send(send_y, lz - 1, sems.at[0, step])
            if step < 2:
                wait_send(ret_y.at[step], nrow - 1, sems.at[4, step])

        @pl.when(others)
        def _():
            wait_send(send_y, lz, sems.at[0, step])

        wait_send(send_z, ncol - 1, sems.at[2, step])
        if step < 2:
            wait_send(ret_z.at[step], ncol - 1, sems.at[6, step])

    def wait_y(step):
        @pl.when(owns)
        def _():
            wait_recv(res_y.at[step], lz - 1, sems.at[5, step])

        @pl.when(others)
        def _():
            wait_recv(res_y.at[step], lz, sems.at[5, step])

    def wait_z(step):
        wait_recv(res_z.at[step], ncol - 1, sems.at[7, step])

    scatter_y(2)
    scatter_z(2)

    chunk = 96 if cells % 96 == 0 else 8

    def x_setup(c, _):
        at = pl.multiple_of(c * chunk, 8)
        excess = recip[pl.ds(at, chunk), :]
        lane = lax.broadcasted_iota(jnp.int32, excess.shape, 1)
        low = jnp.where(lane == 0, 0.0, 1.0)
        up = jnp.where(lane == nx - 1, 0.0, 1.0)

        def keep(slot, values):
            xfac[slot, pl.ds(at, chunk), :] = values

        cyclic_setup(low, up, excess + (1.0 - up), 1, keep)
        return 0

    lax.fori_loop(0, cells // chunk, x_setup, 0)

    lane = lax.broadcasted_iota(jnp.int32, (cells, nx), 1)

    def before_x(values):
        return jnp.where(lane == 0, 0.0, roll(values, 1, 1))

    def after_x(values):
        return jnp.where(lane == nx - 1, 0.0, roll(values, nx - 1, 1))

    def before_y(values, first, shifted):
        shifted[...] = roll(values, 1, 0)
        put_y(shifted, 0, first)
        return shifted[...]

    def after_y(values, last, shifted):
        shifted[...] = roll(values, cells - 1, 0)
        put_y(shifted, ly - 1, last)
        return shifted[...]

    def before_z(values, first):
        return jnp.concatenate([first, values[: cells - ly]], axis=0)

    def after_z(values, last):
        return jnp.concatenate([values[ly:], last], axis=0)

    def x_solve(f_ref, write):
        def lines(c, _):
            at = pl.multiple_of(c * chunk, 8)
            solved = cyclic_solve(
                f_ref[pl.ds(at, chunk), :], 1, lambda slot: xfac[slot, pl.ds(at, chunk), :]
            )
            column = lax.broadcasted_iota(jnp.int32, solved.shape, 1)
            ahead = jnp.where(column == nx - 1, 0.0, roll(solved, nx - 1, 1)) - solved
            write(pl.ds(at, chunk), solved, ahead)
            return 0

        lax.fori_loop(0, cells // chunk, lines, 0)

    zero_y = jnp.zeros((lz, nx), jnp.float32)
    zero_z = jnp.zeros((ly, nx), jnp.float32)

    mz_v = mz[...]
    ey_v = ey[...]
    ay_v = mz_v * inv_half - (after_x(ey_v) - ey_v)
    ay[...] = ay_v
    halos[0].wait_recv()
    my_v = my[...]
    my_before = before_z(my_v, halo_my[...] * gate_c)
    gx_v = keepf[...] * ex[...] - (my_v - my_before) * inv_half
    gx[...] = gx_v
    fx[...] = gx_v + (ay_v - before_y(ay_v, zero_y, sh0))
    rhs_forward(ly, row_y, fx, uy, ry, vy, send_y0, -row_y(ay, ly - 1))
    scatter_y(0)
    halos[1].wait_recv()
    ez_v = ez[...]
    mx_v = mx[...]
    ez_after = after_y(ez_v, halo_ez[pl.ds(0, lz), :] * gate_r_end, sh1)
    az_v = mx_v * inv_half - (ez_after - ez_v)
    az[...] = az_v
    gy_v = keepf[...] * ey_v - (mz_v - before_x(mz_v)) * inv_half
    gy[...] = gy_v
    fy[...] = gy_v + (az_v - before_z(az_v, zero_z))
    rhs_forward(lz, row_z, fy, uz, rz, vz, send_z0, -row_z(az, lz - 1))
    scatter_z(0)

    own_factors()
    halos[2].wait_recv()
    halos[3].wait_recv()
    ex_v = ex[...]
    ax_v = my[...] * inv_half - (after_z(ex_v, halo_ex[...] * gate_c_end) - ex_v)
    ax[...] = ax_v
    mx_v = mx[...]
    mx_before = before_y(mx_v, halo_mx[pl.ds(0, lz), :] * gate_r, sh2)
    gz_v = keepf[...] * ez[...] - (mx_v - mx_before) * inv_half
    gz[...] = gz_v
    fz[...] = gz_v + (ax_v - before_x(ax_v))

    def keep_half(at, solved, ahead):
        ez1[at, :] = solved
        dez[at, :] = ahead

    x_solve(fz, keep_half)
    cz_v = ax[...] + 2.0 * dez[...]
    cz[...] = cz_v
    fz[...] = twice[...] * ez1[...] - gz[...]
    fx[...] = (before_z(cz_v, zero_z) - cz_v) - gx[...]

    own_y(0)
    own_z(0)
    wait_z(0)
    back(lz, put_z, uz, rz, vz, res_z.at[0], ey1, dey)
    cy_v = az[...] + 2.0 * dey[...]
    cy[...] = cy_v
    fz[...] = fz[...] - (cy_v - before_y(cy_v, zero_y, sh1))
    rhs_forward(ly, row_y, fz, uy, ry, wy, send_y1, row_y(cy, ly - 1))
    scatter_y(1)

    wait_y(0)
    back(ly, put_y, uy, ry, vy, res_y.at[0], ex1, dex)
    cx[...] = ay[...] + 2.0 * dex[...]
    fx[...] = fx[...] + twice[...] * ex1[...]
    rhs_forward(lz, row_z, fx, uz, rz, vz, send_z1, row_z(cz, lz - 1))
    scatter_z(1)

    cx_v = cx[...]
    fy[...] = (twice[...] * ey1[...] - gy[...]) - (cx_v - before_x(cx_v))

    def write_y(at, solved, ahead):
        ney[at, :] = solved
        nhz[at, :] = (cx[at, :] - ahead) * half_step

    x_solve(fy, write_y)
    store(1, 5)

    own_y(1)
    own_z(1)
    wait_z(1)
    back(lz, put_z, uz, rz, vz, res_z.at[1], nex, dez)
    nhy[...] = (cz[...] - dez[...]) * half_step
    store(0, 4)
    wait_y(1)
    back(ly, put_y, uy, ry, wy, res_y.at[1], nez, dex)
    nhx[...] = (cy[...] - dex[...]) * half_step
    store(2, 3)
    for step in range(3):
        wait_sent(step)
    for halo in halos:
        halo.wait_send()
    for done in stores:
        done.wait()


def deliver(*refs):
    made, placed, held = refs[:6], refs[6:12], refs[12:18]
    in_sem, out_sem = refs[18], refs[19]
    fetches = [
        pltpu.make_async_copy(made[i], held[i], in_sem.at[i]) for i in range(6)
    ]
    puts = [
        pltpu.make_async_copy(held[i], placed[i], out_sem.at[i]) for i in range(6)
    ]
    for fetch in fetches:
        fetch.start()
    for fetch, put in zip(fetches, puts):
        fetch.wait()
        put.start()
    for put in puts:
        put.wait()


def solution(mesh):
    nrow, ncol = mesh.shape["row"], mesh.shape["col"]

    def per_device(ex, ey, ez, mx, my, mz, tissue, permittivity, conductivity):
        lz, ly, nx = ex.shape
        cells, nt = lz * ly, permittivity.shape[0]
        f32 = jnp.float32
        flat = [a.reshape(cells, nx) for a in (ex, ey, ez, mx, my, mz, tissue)]
        whole = pltpu.VMEM((cells, nx), f32)
        pad_z = -(-lz // 8) * 8
        slots = lambda n: 2 * levels_of(n) + 1
        scratch = (
            [pltpu.SMEM((nt,), f32)] * 2
            + [whole] * 6
            + [pltpu.VMEM((cells, nx), jnp.int32)]
            + [whole] * 31
            + [pltpu.VMEM((slots(nx), cells, nx), f32)]
            + [pltpu.VMEM((ly - 1, lz, nx), f32)] * 4
            + [pltpu.VMEM((lz - 1, ly, nx), f32)] * 3
            + [pltpu.VMEM((lz, TILE, nx), f32)] * 3 + [pltpu.VMEM((ly, TILE, nx), f32)] * 3
            + [pltpu.VMEM((3, nrow, TILE, nx), f32), pltpu.VMEM((3, ncol, TILE, nx), f32)]
            + [pltpu.VMEM((2, nrow, TILE, nx), f32), pltpu.VMEM((2, ncol, TILE, nx), f32)]
            + [pltpu.VMEM((2, lz, TILE, nx), f32), pltpu.VMEM((2, ly, TILE, nx), f32)]
            + [pltpu.VMEM((slots(nrow), nrow, nx), f32), pltpu.VMEM((slots(ncol), ncol, nx), f32)]
            + [pltpu.VMEM((4, nrow, nx), f32), pltpu.VMEM((4, ncol, nx), f32)]
            + [pltpu.VMEM((pad_z, nx), f32)] * 4
            + [pltpu.VMEM((ly, nx), f32)] * 2
            + [
                pltpu.SemaphoreType.DMA((9,)),
                pltpu.SemaphoreType.DMA((6,)),
                pltpu.SemaphoreType.DMA((4,)),
                pltpu.SemaphoreType.DMA((4,)),
                pltpu.SemaphoreType.DMA((8, 3)),
            ]
        )
        outs = pl.pallas_call(
            functools.partial(kernel, (lz, ly, nx, nrow, ncol, nt)),
            out_shape=[jax.ShapeDtypeStruct((cells, nx), f32)] * 6,
            in_specs=[pl.BlockSpec(memory_space=pltpu.HBM)] * 9,
            out_specs=[pl.BlockSpec(memory_space=pltpu.HBM)] * 6,
            scratch_shapes=scratch,
            compiler_params=pltpu.CompilerParams(
                collective_id=0, has_side_effects=True, vmem_limit_bytes=VMEM_BYTES
            ),
        )(*flat, permittivity, conductivity)
        outs = pl.pallas_call(
            deliver,
            out_shape=[jax.ShapeDtypeStruct((cells, nx), f32)] * 6,
            in_specs=[pl.BlockSpec(memory_space=pltpu.HBM)] * 6,
            out_specs=[pl.BlockSpec(memory_space=pltpu.HBM)] * 6,
            scratch_shapes=[whole] * 6 + [pltpu.SemaphoreType.DMA((6,))] * 2,
            compiler_params=pltpu.CompilerParams(vmem_limit_bytes=VMEM_BYTES),
        )(*outs)
        return tuple(o.reshape(lz, ly, nx) for o in outs)

    cut = P("col", "row", None)
    return jax.shard_map(
        per_device,
        mesh=mesh,
        in_specs=(cut,) * 7 + (P(), P()),
        out_specs=(cut,) * 6,
        check_vma=False,
    )
```

```python
import functools

import jax
import jax.numpy as jnp
from jax import lax
from jax.experimental import pallas as pl
from jax.experimental.pallas import tpu as pltpu
from jax.sharding import PartitionSpec as P

MESH = pl.DeviceIdType.MESH
half_step = 32.0
inv_half = 1.0 / half_step
TILE = 4
VMEM_BYTES = 56 * 1024 * 1024


def roll(values, shift, axis):
    return pltpu.roll(values, shift, axis)


def cyclic_setup(low, up, excess, axis, keep):
    n = excess.shape[axis]
    stride = 1
    level = 0
    while stride < n:
        inv = 1.0 / (low + up + excess)
        from_low = low * roll(inv, stride, axis)
        from_up = up * roll(inv, n - stride, axis)
        excess = (
            excess
            + from_low * roll(excess, stride, axis)
            + from_up * roll(excess, n - stride, axis)
        )
        if 2 * stride < n:
            low = from_low * roll(low, stride, axis)
            up = from_up * roll(up, n - stride, axis)
        keep(2 * level, from_low)
        keep(2 * level + 1, from_up)
        stride, level = 2 * stride, level + 1
    keep(2 * level, 1.0 / excess)


def cyclic_solve(rhs, axis, kept):
    n = rhs.shape[axis]
    stride = 1
    level = 0
    while stride < n:
        rhs = (
            rhs
            + kept(2 * level) * roll(rhs, stride, axis)
            + kept(2 * level + 1) * roll(rhs, n - stride, axis)
        )
        stride, level = 2 * stride, level + 1
    return rhs * kept(2 * level)


def levels_of(n):
    return (n - 1).bit_length()


def kernel(sizes, *refs):
    lz, ly, nx, nrow, ncol, nt = sizes
    cells = lz * ly
    (ex_h, ey_h, ez_h, mx_h, my_h, mz_h, tis_h, eps_h, sig_h) = refs[:9]
    outs_h = refs[9:15]
    (
        eps_s, sig_s,
        ex, ey, ez, mx, my, mz, tis,
        nex, ney, nez, nhx, nhy, nhz,
        recip, keepf, twice, gx, gy, gz, ax, ay, az,
        fx, fy, fz, ex1, ey1, ez1, dex, dey, dez, cx, cy, cz,
        sh0, sh1, sh2, sh3,
        xfac,
        uy, ry, vy, wy, uz, rz, vz,
        send_y0, send_y1, send_ym, send_z0, send_z1, send_zm, gat_y, gat_z, ret_y, ret_z, res_y, res_z,
        fac_y, fac_z, mid_y, mid_z,
        halo_mx_s, halo_ez_s, halo_mx, halo_ez, halo_my, halo_ex,
        load_sem, store_sem, halo_send, halo_recv, sems,
    ) = refs[15:]

    me_r, me_c = lax.axis_index("row"), lax.axis_index("col")
    gate_r = jnp.where(me_r > 0, 1.0, 0.0)
    gate_c = jnp.where(me_c > 0, 1.0, 0.0)
    gate_r_end = jnp.where(me_r < nrow - 1, 1.0, 0.0)
    gate_c_end = jnp.where(me_c < ncol - 1, 1.0, 0.0)

    def at_row(p):
        return (p, me_c)

    def at_col(p):
        return (me_r, p)

    barrier = pltpu.get_barrier_semaphore()

    def greet_row(i, _):
        pl.semaphore_signal(
            barrier, inc=1, device_id=at_row(lax.rem(me_r + 1 + i, nrow)), device_id_type=MESH
        )
        return 0

    def greet_col(i, _):
        pl.semaphore_signal(
            barrier, inc=1, device_id=at_col(lax.rem(me_c + 1 + i, ncol)), device_id_type=MESH
        )
        return 0

    lax.fori_loop(0, nrow - 1, greet_row, 0)
    lax.fori_loop(0, ncol - 1, greet_col, 0)

    loads = [
        pltpu.make_async_copy(src, dst, load_sem.at[i])
        for i, (src, dst) in enumerate(
            (
                (eps_h, eps_s),
                (sig_h, sig_s),
                (tis_h, tis),
                (mx_h, mx),
                (ez_h, ez),
                (my_h, my),
                (ex_h, ex),
                (ey_h, ey),
                (mz_h, mz),
            )
        )
    ]
    for load in loads:
        load.start()

    stores = [
        pltpu.make_async_copy(src, dst, store_sem.at[i])
        for i, (src, dst) in enumerate(zip((nex, ney, nez, nhx, nhy, nhz), outs_h))
    ]

    def store(*which):
        for i in which:
            stores[i].start()

    for load in loads[:3]:
        load.wait()
    part = cells // 2
    group = 4

    def look_up(c, _):
        at = pl.ds(pl.multiple_of(c * part, 8), part)
        label = tis[at, :]

        def tissues(g, carry):
            eps, sig = carry
            for j in range(group):
                t = g * group + j
                same = label == t
                eps = jnp.where(same, eps_s[t], eps)
                sig = jnp.where(same, sig_s[t], sig)
            return eps, sig

        zero = jnp.zeros(label.shape, jnp.float32)
        eps, sig = lax.fori_loop(0, nt // group, tissues, (zero, zero))
        loss = sig * (0.5 * half_step)
        scale = inv_half * inv_half
        recip[at, :] = (eps + loss) * scale
        keepf[at, :] = (eps - loss) * scale
        twice[at, :] = eps * (2.0 * scale)
        return 0

    lax.fori_loop(0, 2, look_up, 0)

    for load in loads[3:]:
        load.wait()

    def row_y(ref, i):
        return ref[pl.ds(i, lz, stride=ly), :]

    def put_y(ref, i, values):
        ref[pl.ds(i, lz, stride=ly), :] = values

    def row_z(ref, i):
        return ref[pl.ds(i * ly, ly), :]

    def put_z(ref, i, values):
        ref[pl.ds(i * ly, ly), :] = values

    def matrix_forward(n, row, gate, u_ref, r_ref, send):
        share = row(recip, 0)
        rest = share + gate
        inv = 1.0 / (1.0 + rest)
        reach = inv
        gain = share * inv
        beta, gains = reach, gain
        u_ref[0], r_ref[0] = reach, inv
        for i in range(1, n - 1):
            share = row(recip, i)
            rest = share + rest * inv
            inv = 1.0 / (1.0 + rest)
            gain = (share + gain) * inv
            gains = gains + reach * gain
            further = reach * inv
            beta = beta + reach * further
            reach = further
            u_ref[i], r_ref[i] = reach, inv
        send[:, 0, :] = row(recip, n - 1) + gain
        send[:, 1, :] = gains
        send[:, 2, :] = reach
        send[:, 3, :] = beta

    matrix_forward(ly, row_y, gate_r, uy, ry, send_ym)
    matrix_forward(lz, row_z, gate_c, uz, rz, send_zm)

    halo_mx_s[pl.ds(0, lz), :] = row_y(mx, ly - 1)
    halo_ez_s[pl.ds(0, lz), :] = row_y(ez, 0)
    pl.semaphore_wait(barrier, nrow + ncol - 2)

    up_r, down_r = lax.rem(me_r + 1, nrow), lax.rem(me_r + nrow - 1, nrow)
    up_c, down_c = lax.rem(me_c + 1, ncol), lax.rem(me_c + ncol - 1, ncol)

    def remote(src, dst, send_sem, recv_sem, device):
        return pltpu.make_async_remote_copy(
            src_ref=src,
            dst_ref=dst,
            send_sem=send_sem,
            recv_sem=recv_sem,
            device_id=device,
            device_id_type=MESH,
        )

    halos = [
        remote(my.at[pl.ds(cells - ly, ly), :], halo_my, halo_send.at[0], halo_recv.at[0], at_col(up_c)),
        remote(halo_ez_s, halo_ez, halo_send.at[1], halo_recv.at[1], at_row(down_r)),
        remote(halo_mx_s, halo_mx, halo_send.at[2], halo_recv.at[2], at_row(up_r)),
        remote(ex.at[pl.ds(0, ly), :], halo_ex, halo_send.at[3], halo_recv.at[3], at_col(down_c)),
    ]
    for halo in halos:
        halo.start()

    def rhs_forward(n, row, f_ref, u_ref, r_ref, v_ref, send, passed_on):
        value = row(f_ref, 0) * r_ref[0]
        psi = value
        v_ref[0] = value
        for i in range(1, n - 1):
            value = (row(f_ref, i) + value) * r_ref[i]
            psi = psi + u_ref[i - 1] * value
            v_ref[i] = value
        send[:, 0, :] = row(f_ref, n - 1) + value
        send[:, 1, :] = psi
        send[:, 2, :] = passed_on

    def back(n, row_put, u_ref, r_ref, v_ref, got, out, diff):
        before = got[:, 0, :]
        value = got[:, 1, :]
        row_put(out, n - 1, value)
        row_put(diff, n - 1, got[:, 2, :] - value)
        for i in range(n - 2, -1, -1):
            lower = (v_ref[i] + u_ref[i] * before) + r_ref[i] * value
            row_put(out, i, lower)
            row_put(diff, i, value - lower)
            value = lower


    me_owner_j = lax.div(lz * me_r + nrow - 1, nrow)

    def owner_of(j):
        return lax.div(j * nrow, lz)

    owns = jnp.logical_and(me_owner_j < lz, owner_of(me_owner_j) == me_r)
    others = jnp.logical_not(owns)

    def for_each(count, body):
        half = count // 2

        for k in range(half):
            body(half + k, 0)
            body(half - 1 - k, 0)
        if count % 2:
            body(count - 1, 0)

    def tile(ref, i):
        return ref.at[i]

    def wait_send(ref, count, sem):
        part_of = ref.at[pl.ds(0, count)]
        remote(part_of, part_of, sem, sem, at_row(up_r)).wait_send()

    def wait_recv(ref, count, sem):
        part_of = ref.at[pl.ds(0, count)]
        remote(part_of, part_of, sem, sem, at_row(up_r)).wait_recv()

    sends_y, sends_z = (send_y0, send_y1, send_ym), (send_z0, send_z1, send_zm)

    def scatter_y(step):
        send_y = sends_y[step]

        def to_owner(i, _):
            j, owner = i, i * nrow // lz

            @pl.when(owner != me_r)
            def _():
                remote(
                    tile(send_y, j), tile(gat_y.at[step], me_r), sems.at[0, step], sems.at[1, step], at_row(owner)
                ).start()

            return 0

        for_each(lz, to_owner)

        @pl.when(owns)
        def _():
            gat_y[step, me_r] = send_y[me_owner_j]

    def scatter_z(step):
        send_z = sends_z[step]

        def to_owner(i, _):
            q = jnp.bitwise_and(me_c + 1 + i, ncol - 1) if ncol & (ncol - 1) == 0 else lax.rem(me_c + 1 + i, ncol)
            remote(
                tile(send_z, q), tile(gat_z.at[step], me_c), sems.at[2, step], sems.at[3, step], at_col(q)
            ).start()
            return 0

        for_each(ncol - 1, to_owner)
        gat_z[step, me_c] = send_z[me_c]

    def factor_owned(n, got, fac, mid):
        def read(r):
            return got[2, :, r, :]

        place = lax.broadcasted_iota(jnp.int32, (n, nx), 0)
        starts, ends = place == 0, place == n - 1
        beta = read(3)
        link = jnp.where(starts, 0.0, read(2))
        beta_up = jnp.where(ends, 0.0, roll(beta, n - 1, 0))
        link_up = jnp.where(ends, 0.0, roll(link, n - 1, 0))
        mid[0], mid[1], mid[2], mid[3] = beta, link, beta_up, link_up

        def keep(slot, values):
            fac[slot] = values

        excess = read(0) + jnp.where(ends, 1.0, roll(read(1), n - 1, 0))
        cyclic_setup(link, link_up, excess, 0, keep)

    def solve_owned(step, n, got, fac, mid, ret):
        def read(r):
            return got[step, :, r, :]

        place = lax.broadcasted_iota(jnp.int32, (n, nx), 0)
        starts, ends = place == 0, place == n - 1
        beta, link, beta_up, link_up = mid[0], mid[1], mid[2], mid[3]
        added = jnp.where(starts, 0.0, roll(read(2), 1, 0))
        phi = read(0) + link * added
        psi = read(1) + beta * added
        psi_up = jnp.where(ends, 0.0, roll(psi, n - 1, 0))
        last = cyclic_solve(phi + psi_up, 0, lambda slot: fac[slot])
        before = jnp.where(starts, 0.0, roll(last, 1, 0)) + added
        after = psi_up + beta_up * last + link_up * roll(last, n - 1, 0)
        ret[step, :, 0, :] = before
        ret[step, :, 1, :] = last
        ret[step, :, 2, :] = after

    def own_factors():
        wait_recv(gat_z.at[2], ncol - 1, sems.at[3, 2])
        factor_owned(ncol, gat_z, fac_z, mid_z)

        @pl.when(owns)
        def _():
            wait_recv(gat_y.at[2], nrow - 1, sems.at[1, 2])
            factor_owned(nrow, gat_y, fac_y, mid_y)

    def own_y(step):
        @pl.when(owns)
        def _():
            wait_recv(gat_y.at[step], nrow - 1, sems.at[1, step])
            solve_owned(step, nrow, gat_y, fac_y, mid_y, ret_y)

            def give(i, _):
                q = jnp.bitwise_and(me_r + 1 + i, nrow - 1) if nrow & (nrow - 1) == 0 else lax.rem(me_r + 1 + i, nrow)
                remote(
                    tile(ret_y.at[step], q), tile(res_y.at[step], me_owner_j), sems.at[4, step], sems.at[5, step], at_row(q)
                ).start()
                return 0

            for_each(nrow - 1, give)
            res_y[step, me_owner_j] = ret_y[step, me_r]

    def own_z(step):
        wait_recv(gat_z.at[step], ncol - 1, sems.at[3, step])
        solve_owned(step, ncol, gat_z, fac_z, mid_z, ret_z)

        def give(i, _):
            q = jnp.bitwise_and(me_c + 1 + i, ncol - 1) if ncol & (ncol - 1) == 0 else lax.rem(me_c + 1 + i, ncol)
            remote(
                tile(ret_z.at[step], q), tile(res_z.at[step], me_c), sems.at[6, step], sems.at[7, step], at_col(q)
            ).start()
            return 0

        for_each(ncol - 1, give)
        res_z[step, me_c] = ret_z[step, me_c]

    def wait_sent(step):
        send_y, send_z = sends_y[step], sends_z[step]

        @pl.when(owns)
        def _():
            wait_send(send_y, lz - 1, sems.at[0, step])
            if step < 2:
                wait_send(ret_y.at[step], nrow - 1, sems.at[4, step])

        @pl.when(others)
        def _():
            wait_send(send_y, lz, sems.at[0, step])

        wait_send(send_z, ncol - 1, sems.at[2, step])
        if step < 2:
            wait_send(ret_z.at[step], ncol - 1, sems.at[6, step])

    def wait_y(step):
        @pl.when(owns)
        def _():
            wait_recv(res_y.at[step], lz - 1, sems.at[5, step])

        @pl.when(others)
        def _():
            wait_recv(res_y.at[step], lz, sems.at[5, step])

    def wait_z(step):
        wait_recv(res_z.at[step], ncol - 1, sems.at[7, step])

    scatter_y(2)
    scatter_z(2)

    chunk = 96 if cells % 96 == 0 else 8

    def x_setup(c, _):
        at = pl.multiple_of(c * chunk, 8)
        excess = recip[pl.ds(at, chunk), :]
        lane = lax.broadcasted_iota(jnp.int32, excess.shape, 1)
        low = jnp.where(lane == 0, 0.0, 1.0)
        up = jnp.where(lane == nx - 1, 0.0, 1.0)

        def keep(slot, values):
            xfac[slot, pl.ds(at, chunk), :] = values

        cyclic_setup(low, up, excess + (1.0 - up), 1, keep)
        return 0

    lax.fori_loop(0, cells // chunk, x_setup, 0)

    lane = lax.broadcasted_iota(jnp.int32, (cells, nx), 1)

    def before_x(values):
        return jnp.where(lane == 0, 0.0, roll(values, 1, 1))

    def after_x(values):
        return jnp.where(lane == nx - 1, 0.0, roll(values, nx - 1, 1))

    def before_y(values, first, shifted):
        shifted[...] = roll(values, 1, 0)
        put_y(shifted, 0, first)
        return shifted[...]

    def after_y(values, last, shifted):
        shifted[...] = roll(values, cells - 1, 0)
        put_y(shifted, ly - 1, last)
        return shifted[...]

    def before_z(values, first):
        return jnp.concatenate([first, values[: cells - ly]], axis=0)

    def after_z(values, last):
        return jnp.concatenate([values[ly:], last], axis=0)

    def x_solve(f_ref, write):
        def lines(c, _):
            at = pl.multiple_of(c * chunk, 8)
            solved = cyclic_solve(
                f_ref[pl.ds(at, chunk), :], 1, lambda slot: xfac[slot, pl.ds(at, chunk), :]
            )
            column = lax.broadcasted_iota(jnp.int32, solved.shape, 1)
            ahead = jnp.where(column == nx - 1, 0.0, roll(solved, nx - 1, 1)) - solved
            write(pl.ds(at, chunk), solved, ahead)
            return 0

        lax.fori_loop(0, cells // chunk, lines, 0)

    zero_y = jnp.zeros((lz, nx), jnp.float32)
    zero_z = jnp.zeros((ly, nx), jnp.float32)

    mz_v = mz[...]
    ey_v = ey[...]
    ay_v = mz_v * inv_half - (after_x(ey_v) - ey_v)
    ay[...] = ay_v
    halos[0].wait_recv()
    my_v = my[...]
    my_before = before_z(my_v, halo_my[...] * gate_c)
    gx_v = keepf[...] * ex[...] - (my_v - my_before) * inv_half
    gx[...] = gx_v
    fx[...] = gx_v + (ay_v - before_y(ay_v, zero_y, sh0))
    rhs_forward(ly, row_y, fx, uy, ry, vy, send_y0, -row_y(ay, ly - 1))
    scatter_y(0)
    halos[1].wait_recv()
    ez_v = ez[...]
    mx_v = mx[...]
    ez_after = after_y(ez_v, halo_ez[pl.ds(0, lz), :] * gate_r_end, sh1)
    az_v = mx_v * inv_half - (ez_after - ez_v)
    az[...] = az_v
    gy_v = keepf[...] * ey_v - (mz_v - before_x(mz_v)) * inv_half
    gy[...] = gy_v
    fy[...] = gy_v + (az_v - before_z(az_v, zero_z))
    rhs_forward(lz, row_z, fy, uz, rz, vz, send_z0, -row_z(az, lz - 1))
    scatter_z(0)

    own_factors()
    halos[2].wait_recv()
    halos[3].wait_recv()
    ex_v = ex[...]
    ax_v = my[...] * inv_half - (after_z(ex_v, halo_ex[...] * gate_c_end) - ex_v)
    ax[...] = ax_v
    mx_v = mx[...]
    mx_before = before_y(mx_v, halo_mx[pl.ds(0, lz), :] * gate_r, sh2)
    gz_v = keepf[...] * ez[...] - (mx_v - mx_before) * inv_half
    gz[...] = gz_v
    fz[...] = gz_v + (ax_v - before_x(ax_v))

    def keep_half(at, solved, ahead):
        ez1[at, :] = solved
        dez[at, :] = ahead

    x_solve(fz, keep_half)
    cz_v = ax[...] + 2.0 * dez[...]
    cz[...] = cz_v
    fz[...] = twice[...] * ez1[...] - gz[...]
    fx[...] = (before_z(cz_v, zero_z) - cz_v) - gx[...]

    own_y(0)
    own_z(0)
    wait_z(0)
    back(lz, put_z, uz, rz, vz, res_z.at[0], ey1, dey)
    cy_v = az[...] + 2.0 * dey[...]
    cy[...] = cy_v
    fz[...] = fz[...] - (cy_v - before_y(cy_v, zero_y, sh1))
    rhs_forward(ly, row_y, fz, uy, ry, wy, send_y1, row_y(cy, ly - 1))
    scatter_y(1)

    wait_y(0)
    back(ly, put_y, uy, ry, vy, res_y.at[0], ex1, dex)
    cx[...] = ay[...] + 2.0 * dex[...]
    fx[...] = fx[...] + twice[...] * ex1[...]
    rhs_forward(lz, row_z, fx, uz, rz, vz, send_z1, row_z(cz, lz - 1))
    scatter_z(1)

    cx_v = cx[...]
    fy[...] = (twice[...] * ey1[...] - gy[...]) - (cx_v - before_x(cx_v))

    def write_y(at, solved, ahead):
        ney[at, :] = solved
        nhz[at, :] = (cx[at, :] - ahead) * half_step

    x_solve(fy, write_y)
    store(1, 5)

    own_y(1)
    own_z(1)
    wait_z(1)
    back(lz, put_z, uz, rz, vz, res_z.at[1], nex, dez)
    nhy[...] = (cz[...] - dez[...]) * half_step
    store(0, 4)
    wait_y(1)
    back(ly, put_y, uy, ry, wy, res_y.at[1], nez, dex)
    nhx[...] = (cy[...] - dex[...]) * half_step
    store(2, 3)
    for step in range(3):
        wait_sent(step)
    for halo in halos:
        halo.wait_send()
    for done in stores:
        done.wait()


def deliver(*refs):
    made, placed, held = refs[:6], refs[6:12], refs[12:18]
    in_sem, out_sem = refs[18], refs[19]
    fetches = [
        pltpu.make_async_copy(made[i], held[i], in_sem.at[i]) for i in range(6)
    ]
    puts = [
        pltpu.make_async_copy(held[i], placed[i], out_sem.at[i]) for i in range(6)
    ]
    for fetch in fetches:
        fetch.start()
    for fetch, put in zip(fetches, puts):
        fetch.wait()
        put.start()
    for put in puts:
        put.wait()


def solution(mesh):
    nrow, ncol = mesh.shape["row"], mesh.shape["col"]

    def per_device(ex, ey, ez, mx, my, mz, tissue, permittivity, conductivity):
        lz, ly, nx = ex.shape
        cells, nt = lz * ly, permittivity.shape[0]
        f32 = jnp.float32
        flat = [a.reshape(cells, nx) for a in (ex, ey, ez, mx, my, mz, tissue)]
        whole = pltpu.VMEM((cells, nx), f32)
        pad_z = -(-lz // 8) * 8
        slots = lambda n: 2 * levels_of(n) + 1
        scratch = (
            [pltpu.SMEM((nt,), f32)] * 2
            + [whole] * 6
            + [pltpu.VMEM((cells, nx), jnp.int32)]
            + [whole] * 31
            + [pltpu.VMEM((slots(nx), cells, nx), f32)]
            + [pltpu.VMEM((ly - 1, lz, nx), f32)] * 4
            + [pltpu.VMEM((lz - 1, ly, nx), f32)] * 3
            + [pltpu.VMEM((lz, TILE, nx), f32)] * 3 + [pltpu.VMEM((ly, TILE, nx), f32)] * 3
            + [pltpu.VMEM((3, nrow, TILE, nx), f32), pltpu.VMEM((3, ncol, TILE, nx), f32)]
            + [pltpu.VMEM((2, nrow, TILE, nx), f32), pltpu.VMEM((2, ncol, TILE, nx), f32)]
            + [pltpu.VMEM((2, lz, TILE, nx), f32), pltpu.VMEM((2, ly, TILE, nx), f32)]
            + [pltpu.VMEM((slots(nrow), nrow, nx), f32), pltpu.VMEM((slots(ncol), ncol, nx), f32)]
            + [pltpu.VMEM((4, nrow, nx), f32), pltpu.VMEM((4, ncol, nx), f32)]
            + [pltpu.VMEM((pad_z, nx), f32)] * 4
            + [pltpu.VMEM((ly, nx), f32)] * 2
            + [
                pltpu.SemaphoreType.DMA((9,)),
                pltpu.SemaphoreType.DMA((6,)),
                pltpu.SemaphoreType.DMA((4,)),
                pltpu.SemaphoreType.DMA((4,)),
                pltpu.SemaphoreType.DMA((8, 3)),
            ]
        )
        outs = pl.pallas_call(
            functools.partial(kernel, (lz, ly, nx, nrow, ncol, nt)),
            out_shape=[jax.ShapeDtypeStruct((cells, nx), f32)] * 6,
            in_specs=[pl.BlockSpec(memory_space=pltpu.HBM)] * 9,
            out_specs=[pl.BlockSpec(memory_space=pltpu.HBM)] * 6,
            scratch_shapes=scratch,
            compiler_params=pltpu.CompilerParams(
                collective_id=0, has_side_effects=True, vmem_limit_bytes=VMEM_BYTES
            ),
        )(*flat, permittivity, conductivity)
        outs = pl.pallas_call(
            deliver,
            out_shape=[jax.ShapeDtypeStruct((cells, nx), f32)] * 6,
            in_specs=[pl.BlockSpec(memory_space=pltpu.HBM)] * 6,
            out_specs=[pl.BlockSpec(memory_space=pltpu.HBM)] * 6,
            scratch_shapes=[whole] * 6 + [pltpu.SemaphoreType.DMA((6,))] * 2,
            compiler_params=pltpu.CompilerParams(vmem_limit_bytes=VMEM_BYTES),
        )(*outs)
        return tuple(o.reshape(lz, ly, nx) for o in outs)

    cut = P("col", "row", None)
    return jax.shard_map(
        per_device,
        mesh=mesh,
        in_specs=(cut,) * 7 + (P(), P()),
        out_specs=(cut,) * 6,
        check_vma=False,
    )
```
